256 devices in a mesh: dp: 32 (over z, y), mp: 8 (over x, core).
Axes of the slice: x: 4, y: 4, z: 8, core: 2. Of those that a mesh axis runs over, the one named last changes fastest.
Arguments:
- queries: bfloat16 [16384, 2048], P('dp', 'mp'), may hold values from -96 to 96
- out_grad: bfloat16 [16384, 2048], P('dp', 'mp'), may hold values from -0.75 to 0.75
- owner: int32 [256, 2], P('dp'), may hold values from 0 to 31, all different within a row; in each aligned block of 8 rows (0 to 7, 8 to 15, ...) at most 2 rows name the same one
- store_row: int32 [256, 2], P('dp'), may hold values from 0 to 1
- store: bfloat16 [64, 128, 4096], P('dp', None, 'mp'), may hold values from -80 to 80
- norm_gain: bfloat16 [4096], P('mp'), may hold values from 0.5 to 2
- w_key: bfloat16 [4096, 2048], P(None, 'mp'), may hold values from -0.09375 to 0.09375
- w_value: bfloat16 [4096, 2048], P(None, 'mp'), may hold values from -0.09375 to 0.09375
Outputs:
- attended: bfloat16 [16384, 2048], P('dp', 'mp')
- query_grad: bfloat16 [16384, 2048], P('dp', 'mp')
- key_weight_grad: float32 [4096, 2048], P('dp', 'mp')
- value_weight_grad: float32 [4096, 2048], P('dp', 'mp')
The draws below stay inside these ranges and needn't reach their ends.
Inputs may be any that keep to these rules, and one draw needn't show every extreme that they name: Within the 8 spans of one index of dp no owner is named more than 2 times, and in some such block one owner is named exactly 2 times; the 2 neighbours of a span have different owners.
All inputs are finite; a program needn't handle non-finite values.
Results may differ from the reference program's by a relative error of at most 0.03.
The reference program's roundings to bfloat16 on the way count: a program that leaves them out, or rounds other values in their place, can miss the bound.
Values may be sent and summed in bfloat16 or wider, within the bound.
A program may use at most 128 MiB of HBM per device.

```python
import math
import jax
import jax.numpy as jnp
import numpy as np
from jax import lax

D = 4096
HEADS = 16
HEAD = 128
SPAN = 64
NLEN = 128
NBR = 2
CH_DEV = 8
STORE_DEV = 2
CAP = 2
SPANS = 256
TOKENS = 16384
STORES = 64
N_DP = 32


def draw_queries(key, part):
    key = jax.random.fold_in(key, 11)
    subkeys = jax.random.split(key, 1)
    shape = (TOKENS, HEADS * HEAD)
    base = jax.random.normal(subkeys[0], shape, jnp.float32) * 2.0
    return jnp.clip(base, -96.0, 96.0).astype(jnp.bfloat16)


def draw_store(key, part):
    key = jax.random.fold_in(key, 23)
    subkeys = jax.random.split(key, 2)
    shape = (STORES, NLEN, D)
    row_scale = jnp.exp(jax.random.uniform(subkeys[1], (STORES, NLEN, 1), jnp.float32, 0.0, 2.302585))
    base = jax.random.normal(subkeys[0], shape, jnp.float32)
    return jnp.clip(base * row_scale, -80.0, 80.0).astype(jnp.bfloat16)


def place_ends(drawn, rng, least, top_value):
    spot = [jax.random.randint(jax.random.fold_in(rng, axis), (), 0, length) for axis, length in enumerate(drawn.shape)]
    widest = drawn.shape.index(max(drawn.shape))
    neighbour = spot[:widest] + [(spot[widest] + 1) % drawn.shape[widest]] + spot[widest + 1:]
    return drawn.at[tuple(spot)].set(least).at[tuple(neighbour)].set(top_value)


def block_levels(stream_key, shape, pieces, least, high):
    factor_of, own = 1.0, jax.random.fold_in(stream_key, 6)
    for dim, blocks in pieces:
        steps = jnp.exp(jax.random.uniform(jax.random.fold_in(own, dim), (blocks,), jnp.float32, least / len(pieces), high / len(pieces)))
        factor_of = factor_of * jnp.repeat(steps, shape[dim] // blocks).reshape([-1 if axis == dim else 1 for axis in range(len(shape))])
    return factor_of


def deal_out(stream_key, own, number, rows, amount, top, limit, lean):
    ranking = jax.random.permutation(stream_key, amount)
    crowded, common = portions_of(amount, rows * top, limit, lean, True), portions_of(amount, rows * top, limit, lean, False)
    places = jnp.arange(amount)

    def named(tallies, rotation):
        used = int((tallies > 0).sum())
        fixed = max(1, used // 4)
        shifted = fixed + (places - fixed + rotation * (used - fixed)) % max(1, amount - fixed)
        return jnp.zeros((amount,), jnp.int32).at[ranking[jnp.where(places < fixed, places, shifted)]].set(jnp.asarray(tallies, jnp.int32))

    tallies = jnp.where(number % 4 == 0, named(crowded, number // 4), named(common, number - number // 4 - 1))
    mixed = jax.random.permutation(jax.random.fold_in(own, 3), amount)
    donor, taker = mixed[0:amount // 2 * 2:2], mixed[1:amount // 2 * 2:2]
    slack = jnp.minimum(tallies[donor] - 1, limit - tallies[taker]) // 2
    slack = jnp.where((donor == ranking[0]) | (taker == ranking[0]) | (tallies[taker] == 0), 0, jnp.maximum(slack, 0))
    shifted = jax.random.randint(jax.random.fold_in(own, 4), (amount // 2,), 0, 1 << 20) % (slack + 1)
    tallies = tallies.at[donor].add(-shifted).at[taker].add(shifted)
    items = jnp.searchsorted(jnp.cumsum(tallies), jnp.arange(rows * top), side="right").astype(jnp.int32)
    grid = items.reshape(top, rows).T
    grid = grid[jax.random.permutation(jax.random.fold_in(own, 1), rows)]
    rotation = jax.random.randint(jax.random.fold_in(own, 2), (rows, 1), 0, top)
    return jnp.take_along_axis(grid, (jnp.arange(top)[None, :] + rotation) % top, axis=1)


def portions_of(number_of, total, bound, skew, full):
    weights = [(1 << 20) // math.isqrt(grade ** skew) + 1 for grade in range(1, number_of + 1)]
    largest = bound if full else min(bound, max(-(-total // number_of), total * weights[0] // sum(weights)))
    least = 1 if total - largest >= number_of - 1 else 0
    given, spare = [largest] + [least] * (number_of - 1), total - largest - least * (number_of - 1)
    while spare > 0:
        movable = [i for i in range(1, number_of) if given[i] < largest] or [i for i in range(1, number_of) if given[i] < bound]
        whole, remaining = sum([weights[i] for i in movable]), spare
        for i in movable:
            addition = min(bound - given[i], max(1, remaining * weights[i] // whole), spare)
            given[i] = given[i] + addition
            spare = spare - addition
    return np.array(given)


def bell_draw(own_key, dims, scale, reach, cuts=(), dtype=jnp.bfloat16):
    drawn = scale * jax.random.normal(own_key, dims, jnp.float32)
    if cuts:
        drawn = drawn * block_levels(own_key, dims, cuts, -0.22, 0.18)
    return jnp.clip(drawn, -reach, reach).astype(dtype)


def setup_inputs(seed: int = 0) -> dict:
    arg_keys = jax.random.split(jax.random.key(seed), 9)
    queries = draw_queries(jax.random.fold_in(arg_keys[8], 71), 0)
    out_grad = bell_draw(arg_keys[1], (TOKENS, HEADS * HEAD), 0.125, 0.75, ((0, 32), (1, 8)))
    owner_keys = jax.random.split(jax.random.fold_in(arg_keys[2], 1), SPANS // CH_DEV)
    owner_turns = jax.random.permutation(jax.random.fold_in(arg_keys[2], 3), SPANS // CH_DEV)
    owner = jax.vmap(lambda own, number: deal_out(jax.random.fold_in(arg_keys[2], 2), own, number, CH_DEV, N_DP, NBR, CAP, 2))(owner_keys, owner_turns).reshape((SPANS, NBR))
    store_row = place_ends(jax.random.randint(arg_keys[3], (SPANS, NBR), 0, STORE_DEV), jax.random.fold_in(arg_keys[3], 1), 0, STORE_DEV - 1).astype(jnp.int32)
    store = draw_store(jax.random.fold_in(arg_keys[8], 71), 0)
    norm_gain = jnp.clip(jnp.exp(math.log(2.0) - 1.3862944 * jax.random.uniform(arg_keys[5], (D,), jnp.float32) ** block_levels(arg_keys[5], (D,), ((0, 8),), -0.2, 0.2)), 0.5, 2.0).astype(jnp.bfloat16)
    w_key = bell_draw(arg_keys[6], (D, HEADS * HEAD), D ** -0.5, 0.09375, ((1, 8),))
    w_value = bell_draw(arg_keys[7], (D, HEADS * HEAD), D ** -0.5, 0.09375, ((1, 8),))
    return dict(queries=queries, out_grad=out_grad, owner=owner, store_row=store_row, store=store, norm_gain=norm_gain, w_key=w_key, w_value=w_value)


epsilon = 1e-06

def reference(queries, out_grad, owner, store_row, store, norm_gain, w_key, w_value):
    model_width = HEADS * HEAD
    floats = store.astype(jnp.float32)
    scale_rows = lax.rsqrt(lax.optimization_barrier(jnp.mean(floats * floats, axis=-1, keepdims=True)) + epsilon)
    normed = (floats * scale_rows * norm_gain.astype(jnp.float32)).astype(jnp.bfloat16).reshape(STORES * NLEN, D)
    key_rows = jnp.dot(normed, w_key, preferred_element_type=jnp.float32).astype(jnp.bfloat16).reshape(STORES, NLEN, model_width)
    value_rows = jnp.dot(normed, w_value, preferred_element_type=jnp.float32).astype(jnp.bfloat16).reshape(STORES, NLEN, model_width)
    inverse_root = 1.0 / math.sqrt(HEAD)
    references = CH_DEV * NBR
    earlier = jnp.tril(jnp.ones((references, references), jnp.float32), -1)
    query_blocks = queries.reshape(N_DP, CH_DEV, SPAN, HEADS, HEAD)
    grad_blocks = out_grad.reshape(N_DP, CH_DEV, SPAN, HEADS, HEAD)
    id_blocks = (owner.astype(jnp.int32) * STORE_DEV + store_row.astype(jnp.int32)).astype(jnp.int32).reshape(N_DP, references)

    def block_step(state_pair, block_args):
        acc_key, acc_value = state_pair
        query_blk, grad_blk, global_id = block_args
        query_f = query_blk.astype(jnp.float32)
        grad_f = grad_blk.astype(jnp.float32)
        key_ctx = jnp.take(key_rows, global_id, axis=0).reshape(CH_DEV, NBR * NLEN, HEADS, HEAD).astype(jnp.float32)
        value_ctx = jnp.take(value_rows, global_id, axis=0).reshape(CH_DEV, NBR * NLEN, HEADS, HEAD).astype(jnp.float32)
        scores = jnp.einsum('cqhd,ckhd->chqk', query_f, key_ctx) * inverse_root
        probs = jax.nn.softmax(scores, axis=-1)
        probs_low = lax.optimization_barrier(probs.astype(jnp.bfloat16)).astype(jnp.float32)
        attended_blk = jnp.einsum('chqk,ckhd->cqhd', probs_low, value_ctx).astype(jnp.bfloat16)
        prob_grad = jnp.einsum('cqhd,ckhd->chqk', grad_f, value_ctx)
        row_delta = lax.optimization_barrier(jnp.sum(probs * prob_grad, axis=-1, keepdims=True))
        score_grad = lax.optimization_barrier((probs * (prob_grad - row_delta)).astype(jnp.bfloat16)).astype(jnp.float32)
        query_grad_blk = (jnp.einsum('chqk,ckhd->cqhd', score_grad, key_ctx) * inverse_root).astype(jnp.bfloat16)
        key_grad = jnp.einsum('chqk,cqhd->ckhd', score_grad, query_f) * inverse_root
        value_grad = jnp.einsum('chqk,cqhd->ckhd', probs_low, grad_f)
        same_id = (global_id[:, None] == global_id[None, :]).astype(jnp.float32)
        first_use = lax.optimization_barrier(jnp.sum(same_id * earlier, axis=1)) == 0.0
        summed_key = jnp.einsum('ij,jtc->itc', same_id, key_grad.reshape(references, NLEN, model_width), precision=lax.Precision.HIGHEST)
        summed_value = jnp.einsum('ij,jtc->itc', same_id, value_grad.reshape(references, NLEN, model_width), precision=lax.Precision.HIGHEST)
        sent_key = lax.optimization_barrier(jnp.where(first_use[:, None, None], summed_key, 0.0).astype(jnp.bfloat16)).astype(jnp.float32)
        sent_value = lax.optimization_barrier(jnp.where(first_use[:, None, None], summed_value, 0.0).astype(jnp.bfloat16)).astype(jnp.float32)
        acc_key = acc_key.at[global_id].add(sent_key)
        acc_value = acc_value.at[global_id].add(sent_value)
        return ((acc_key, acc_value), (attended_blk, query_grad_blk))
    start_grads = (jnp.zeros((STORES, NLEN, model_width), jnp.float32), jnp.zeros((STORES, NLEN, model_width), jnp.float32))
    (sum_key, sum_value), (attended, query_grad) = lax.scan(block_step, start_grads, (query_blocks, grad_blocks, id_blocks))
    row_key = sum_key.astype(jnp.bfloat16).reshape(N_DP, STORE_DEV * NLEN, model_width)
    row_value = sum_value.astype(jnp.bfloat16).reshape(N_DP, STORE_DEV * NLEN, model_width)
    normed_blocks = normed.reshape(N_DP, STORE_DEV * NLEN, D)

    def weight_step(state_pair, block_args):
        normed_blk, key_blk, value_blk = block_args
        key_term = jnp.dot(normed_blk.T, key_blk, preferred_element_type=jnp.float32)
        value_term = jnp.dot(normed_blk.T, value_blk, preferred_element_type=jnp.float32)
        key_term = lax.optimization_barrier(key_term.astype(jnp.bfloat16)).astype(jnp.float32)
        value_term = lax.optimization_barrier(value_term.astype(jnp.bfloat16)).astype(jnp.float32)
        return ((state_pair[0] + key_term, state_pair[1] + value_term), None)
    start_weights = (jnp.zeros((D, model_width), jnp.float32), jnp.zeros((D, model_width), jnp.float32))
    (key_weight_grad, value_weight_grad), unused = lax.scan(weight_step, start_weights, (normed_blocks, row_key, row_value))
    attended = attended.reshape(TOKENS, model_width)
    query_grad = query_grad.reshape(TOKENS, model_width)
    return (attended, query_grad, key_weight_grad, value_weight_grad)
```

```python
import functools
import math

import jax
import jax.numpy as jnp
from jax import lax
from jax.experimental import pallas as pl
from jax.experimental.pallas import tpu as pltpu
from jax.sharding import PartitionSpec as P

MESH = pl.DeviceIdType.MESH
VMEM = pltpu.VMEM
F32, BF16, I32 = jnp.float32, jnp.bfloat16, jnp.int32

HEAD = 128
EPS = 1e-06
NZ, NY, NM = 8, 4, 8
CH = 4
TOK = 32
REFS = 16
GAINROWS = 16
ROWS = 256 + GAINROWS
LIMIT = 56 * 1024 * 1024


def wrap(value, size):
    return lax.rem(value + size, size)


def place():
    d, m = lax.axis_index("dp"), lax.axis_index("mp")
    return lax.div(d, NY), lax.rem(d, NY), m


def remote(src, dst, send, recv, z, y, m):
    return pltpu.make_async_remote_copy(
        src_ref=src, dst_ref=dst, send_sem=send, recv_sem=recv, device_id=(z * NY + y, m), device_id_type=MESH
    )


def greet(peers):
    barrier = pltpu.get_barrier_semaphore()
    for z, y, m in peers:
        pl.semaphore_signal(barrier, inc=1, device_id=(z * NY + y, m), device_id_type=MESH)
    pl.semaphore_wait(barrier, len(peers))


class MpGather:
    def __init__(self, ref, low, high, send, recv):
        self.ref, self.send, self.recv = ref, send, recv
        self.z, self.y, self.m = place()
        self.right, self.left, self.opposite = wrap(self.m + 2, NM), wrap(self.m - 2, NM), wrap(self.m + 4, NM)
        self.twin = self.m + 1 - 2 * lax.rem(self.m, 2)
        self.low, self.high, self.whole = (0, low), (low, high - low), (0, high)

    def copy(self, block, part, target, k):
        piece = self.ref.at[block, pl.ds(*part)]
        return remote(piece, piece, self.send.at[k], self.recv.at[k], self.z, self.y, target)

    def sent(self):
        m, left, right, opposite = self.m, self.left, self.right, self.opposite
        return [
            (m, self.low, right), (m, self.high, right), (m, self.high, left), (m, self.low, left), (m, self.whole, self.twin),
            (left, self.low, right), (right, self.high, left),
            (left, self.whole, self.twin), (right, self.whole, self.twin),
            (opposite, self.low, self.twin), (opposite, self.high, self.twin),
        ]

    def came(self):
        m, left, right, opposite, twin = self.m, self.left, self.right, self.opposite, self.twin
        tl, tr, to = wrap(twin - 2, NM), wrap(twin + 2, NM), wrap(twin + 4, NM)
        return [
            (left, self.low), (left, self.high), (right, self.high), (right, self.low), (twin, self.whole),
            (opposite, self.low), (opposite, self.high),
            (tl, self.whole), (tr, self.whole), (to, self.low), (to, self.high),
        ]

    def start(self, k):
        block, part, target = self.sent()[k]
        self.copy(block, part, target, k).start()

    def arrive(self, k):
        block, part = self.came()[k]
        self.copy(block, part, self.twin, k).wait_recv()

    def finish_send(self, k):
        block, part, target = self.sent()[k]
        self.copy(block, part, target, k).wait_send()

    def step(self, number):
        if number == 0:
            for k in (0, 2, 1, 3, 4):
                self.start(k)
        elif number == 1:
            self.arrive(0)
            self.start(5)
            self.arrive(2)
            self.start(6)
        elif number == 2:
            self.arrive(1)
            self.start(7)
            self.arrive(3)
            self.start(8)
        elif number == 3:
            self.arrive(5)
            self.start(9)
            self.arrive(6)
            self.start(10)
        else:
            for k in (4, 7, 8, 9, 10):
                self.arrive(k)
            for k in range(11):
                self.finish_send(k)

    STEPS = 5


def gather_kernel(store_ref, gain_ref, all_ref, send, recv):
    z, y, m = place()
    moves = MpGather(all_ref, 128, ROWS, send, recv)
    all_ref[m, 0:256] = store_ref[...]
    all_ref[m, 256:ROWS] = jnp.broadcast_to(gain_ref[...], (GAINROWS, 512))
    greet([(z, y, moves.right), (z, y, moves.left), (z, y, moves.twin)])
    for number in range(MpGather.STEPS):
        moves.step(number)


def encode_kernel(all_ref, key_ref, value_ref, kv_ref, turned_ref):
    m = lax.axis_index("mp")
    total = jnp.zeros((256, 1), F32)
    for j in range(NM):
        part = all_ref[j, 0:256].astype(F32)
        total += jnp.sum(part * part, axis=-1, keepdims=True)
    scale = lax.rsqrt(total * (1.0 / 4096.0) + EPS)

    def normed(j):
        gain = all_ref[j, 256:ROWS][0:1].astype(F32)
        return (all_ref[j, 0:256].astype(F32) * scale * gain).astype(BF16)

    keys = jnp.zeros((256, 256), F32)
    values = jnp.zeros((256, 256), F32)
    for j in range(NM):
        block = normed(j)
        keys += jnp.dot(block, key_ref[512 * j : 512 * (j + 1)], preferred_element_type=F32)
        values += jnp.dot(block, value_ref[512 * j : 512 * (j + 1)], preferred_element_type=F32)
    for g in range(4):
        rows = (keys if g < 2 else values)[:, 128 * (g % 2) : 128 * (g % 2) + 128].astype(BF16)
        for n in range(2):
            for t in range(CH):
                first = 128 * n + TOK * t
                kv_ref[g, t, n] = rows[first : first + TOK]
    turned = normed(m).astype(F32).T.astype(BF16)
    for k in range(NY):
        turned_ref[k] = turned[128 * k : 128 * (k + 1)]


def hops(t):
    return (4, 3) if t % 2 == 0 else (3, 4)


def context_kernel(
    kv_ref, turned_ref, owner_ref, row_ref, ctx_ref, normed_ref, table_ref,
    g0, g1, g2, g3, chosen, relay, table_s, near_s, near_r, ring_s, ring_r, out_s, out_r, tab_s, tab_r, turn_s, turn_r, mp_s, mp_r, own_sem,
):
    z, y, m = place()
    chunks = (g0, g1, g2, g3)
    right_y, left_y, far_y = wrap(y + 1, NY), wrap(y - 1, NY), wrap(y + 2, NY)
    up, down = wrap(z + 1, NZ), wrap(z - 1, NZ)
    moves = MpGather(normed_ref, 64, 128, mp_s, mp_r)
    others = (right_y, far_y, left_y)

    ids = owner_ref[...] * 2 + row_ref[...]
    lane = lax.broadcasted_iota(I32, (8, 128), 1)
    span = lax.broadcasted_iota(I32, (8, 128), 0)
    first, second = ids[:, 0:1], ids[:, 1:2]
    match = jnp.minimum(jnp.where(lane == first, 2 * span, REFS), jnp.where(lane == second, 2 * span + 1, REFS))
    table_ref[y, 0:8] = jnp.where(lane == 0, first, second)
    table_ref[y, 8:16] = jnp.broadcast_to(jnp.min(match, axis=0, keepdims=True), (8, 128))

    greet(
        [(z, o, m) for o in others]
        + [(up, y, m), (down, y, m)]
        + [(z, y, moves.right), (z, y, moves.left), (z, y, moves.twin)]
    )

    def near(k, t, source, target):
        return remote(
            kv_ref.at[target, t], chunks[t].at[pl.ds(8 * z + 2 * source, 2)], near_s.at[k, t], near_r.at[k, t], z, target, m
        )

    def tab(k, source, target):
        return remote(table_ref.at[source], table_ref.at[source], tab_s.at[k], tab_r.at[k], z, target, m)

    def turn(k, source, target):
        return remote(
            turned_ref.at[target], normed_ref.at[m, :, pl.ds(pl.multiple_of(256 * source, 256), 256)],
            turn_s.at[k], turn_r.at[k], z, target, m,
        )

    for t in range(CH):
        for k in range(3):
            near(k, t, y, others[k]).start()
    for k in range(3):
        tab(k, y, others[k]).start()
    for k in range(3):
        turn(k, y, others[k]).start()
    for t in range(CH):
        chunks[t][pl.ds(8 * z + 2 * y, 2)] = kv_ref[y, t]
    own_turn = pltpu.make_async_copy(
        turned_ref.at[y], normed_ref.at[m, :, pl.ds(pl.multiple_of(256 * y, 256), 256)], own_sem.at[0]
    )
    own_turn.start()

    def ring(t, direction, h, block, target):
        piece = chunks[t].at[pl.ds(8 * block, 8)]
        return remote(piece, piece, ring_s.at[t, direction, h], ring_r.at[t, direction, h], target, y, m)

    def sender(t, direction, h):
        block = wrap(z - h, NZ) if direction == 0 else wrap(z + h, NZ)
        return ring(t, direction, h, block, up if direction == 0 else down)

    def receiver(t, direction, h):
        block = wrap(z - 1 - h, NZ) if direction == 0 else wrap(z + 1 + h, NZ)
        return ring(t, direction, h, block, up)

    def out(t, k, src, dst, target):
        return remote(src, dst, out_s.at[t, k], out_r.at[t, k], z, target, m)

    def outgoing(t, k):
        if k == 0:
            return out(t, 0, chosen.at[t, 0], ctx_ref.at[y, t], right_y)
        if k == 1:
            return out(t, 1, chosen.at[t, 2], ctx_ref.at[y, t], left_y)
        if k == 2:
            return out(t, 2, chosen.at[t, 1, pl.ds(0, 8)], relay.at[t, 0], right_y)
        if k == 3:
            return out(t, 3, chosen.at[t, 1, pl.ds(8, 8)], relay.at[t, 1], left_y)
        if k == 4:
            return out(t, 4, relay.at[t, 0], ctx_ref.at[left_y, t, pl.ds(0, 8)], right_y)
        return out(t, 5, relay.at[t, 1], ctx_ref.at[right_y, t, pl.ds(8, 8)], left_y)

    def incoming(t, k):
        if k == 0:
            return out(t, 0, chosen.at[t, 0], ctx_ref.at[left_y, t], right_y)
        if k == 1:
            return out(t, 1, chosen.at[t, 2], ctx_ref.at[right_y, t], left_y)
        if k in (2, 3):
            return out(t, k, relay.at[t, k - 2], relay.at[t, k - 2], right_y)
        if k == 4:
            return out(t, 4, relay.at[t, 0], ctx_ref.at[far_y, t, pl.ds(0, 8)], right_y)
        return out(t, 5, relay.at[t, 1], ctx_ref.at[far_y, t, pl.ds(8, 8)], left_y)

    def begin(t):
        for k in range(3):
            near(k, t, wrap(y - 1 - k, NY), y).wait_recv()
        sender(t, 0, 0).start()
        sender(t, 1, 0).start()

    def advance(t, h):
        for direction in (0, 1):
            if h < hops(t)[direction]:
                receiver(t, direction, h).wait_recv()
                if h + 1 < hops(t)[direction]:
                    sender(t, direction, h + 1).start()

    def choose(t):
        if t == 0:
            for k in range(3):
                tab(k, wrap(y - 1 - k, NY), y).wait_recv()
            copy = pltpu.make_async_copy(table_ref, table_s, own_sem.at[1])
            copy.start()
            copy.wait()

        def body(c, carry):
            for n in range(2):
                for k in (2, 1, 3, 0):
                    picked = chunks[t][table_s[wrap(y + k, NY), c, n]]
                    if k == 0:
                        ctx_ref[y, t, 2 * c + n] = picked
                    else:
                        chosen[t, k - 1, 2 * c + n] = picked
            return carry

        lax.fori_loop(0, 8, body, 0)
        for k in (2, 3, 0, 1):
            outgoing(t, k).start()

    def pass_on(t):
        for k in (2, 3):
            incoming(t, k).wait_recv()
            outgoing(t, k + 2).start()

    def begin_mp():
        own_turn.wait()
        for k in range(3):
            turn(k, wrap(y - 1 - k, NY), y).wait_recv()
        moves.step(0)

    events = []
    for t in range(CH):
        events.append((2 * t, 0, functools.partial(begin, t)))
        for h in range(4):
            events.append((2 * t + h + 1, 1, functools.partial(advance, t, h)))
        events.append((2 * t + 4, 2, functools.partial(choose, t)))
        events.append((2 * t + 6, 3, functools.partial(pass_on, t)))
    events.append((1, 4, begin_mp))
    for number in range(1, MpGather.STEPS):
        events.append((2 * number + 4, 4, functools.partial(moves.step, number)))
    for _, _, action in sorted(events, key=lambda event: event[:2]):
        action()
    for t in range(CH):
        for k in (0, 1, 4, 5):
            incoming(t, k).wait_recv()
    for t in range(CH):
        for k in range(6):
            outgoing(t, k).wait_send()
        for k in range(3):
            near(k, t, y, others[k]).wait_send()
        for direction in (0, 1):
            for h in range(hops(t)[direction]):
                sender(t, direction, h).wait_send()
    for k in range(3):
        tab(k, y, others[k]).wait_send()
        turn(k, y, others[k]).wait_send()


def attention_kernel(table_s, q_ref, o_ref, ctx_ref, att_ref, qg_ref, grad_ref, full):
    y = lax.rem(lax.axis_index("dp"), NY)
    root = 1.0 / math.sqrt(HEAD)
    down = (((1,), (1,)), ((), ()))
    across = (((0,), (0,)), ((), ()))
    for c in range(8):
        rows = slice(64 * c, 64 * c + 64)
        for h in range(2):
            columns = slice(128 * h, 128 * h + 128)
            q, o = q_ref[rows, columns], o_ref[rows, columns]
            keys = ctx_ref[h, :, 2 * c : 2 * c + 2].reshape(256, 128)
            values = ctx_ref[2 + h, :, 2 * c : 2 * c + 2].reshape(256, 128)
            scores = lax.dot_general(q, keys, down, preferred_element_type=F32) * root
            weights = jnp.exp(scores - jnp.max(scores, axis=-1, keepdims=True))
            probs = weights / jnp.sum(weights, axis=-1, keepdims=True)
            low = probs.astype(BF16)
            att_ref[rows, columns] = jnp.dot(low, values, preferred_element_type=F32).astype(BF16)
            prob_grad = lax.dot_general(o, values, down, preferred_element_type=F32)
            delta = jnp.sum(probs * prob_grad, axis=-1, keepdims=True)
            score_grad = (probs * (prob_grad - delta)).astype(BF16)
            qg_ref[rows, columns] = (jnp.dot(score_grad, keys, preferred_element_type=F32) * root).astype(BF16)
            key_grad = lax.dot_general(score_grad, q, across, preferred_element_type=F32) * root
            value_grad = lax.dot_general(low, o, across, preferred_element_type=F32)
            for g, grad in ((h, key_grad), (2 + h, value_grad)):
                grad = grad.reshape(CH, 2, TOK, 128)
                full[g, :, 2 * c : 2 * c + 2] = grad
                grad_ref[g, :, 2 * c : 2 * c + 2] = grad.astype(BF16)

    def fold(r, carry):
        first = table_s[y, 8, table_s[y, lax.div(r, 2), lax.rem(r, 2)]]

        @pl.when(first != r)
        def _():
            grad_ref[:, :, first] = (full[:, :, first] + full[:, :, r]).astype(BF16)

        return carry

    lax.fori_loop(0, REFS, fold, 0)


def weight_kernel(
    table_s, grad_ref, normed_ref, key_ref, value_ref,
    r0, r1, r2, r3, relay, dense, ring_up, ring_down, rows, parts, first_up, first_down, sum_up, sum_down,
    out_s, out_r, ring_s, ring_r, near_s, near_r, sum_s, sum_r,
):
    z, y, m = place()
    came = (r0, r1, r2, r3)
    right_y, left_y, far_y = wrap(y + 1, NY), wrap(y - 1, NY), wrap(y + 2, NY)
    up, down = wrap(z + 1, NZ), wrap(z - 1, NZ)
    greet([(z, right_y, m), (z, left_y, m), (up, y, m), (down, y, m)])

    def out(t, k, src, dst, target):
        return remote(src, dst, out_s.at[t, k], out_r.at[t, k], z, target, m)

    def outgoing(t, k):
        if k == 0:
            return out(t, 0, grad_ref.at[right_y, t], came[t].at[y, pl.ds(0, 16)], right_y)
        if k == 1:
            return out(t, 1, grad_ref.at[left_y, t], came[t].at[y, pl.ds(0, 16)], left_y)
        if k == 2:
            return out(t, 2, grad_ref.at[far_y, t, pl.ds(0, 8)], relay.at[t, 0], right_y)
        if k == 3:
            return out(t, 3, grad_ref.at[far_y, t, pl.ds(8, 8)], relay.at[t, 1], left_y)
        if k == 4:
            return out(t, 4, relay.at[t, 0], came[t].at[left_y, pl.ds(0, 8)], right_y)
        return out(t, 5, relay.at[t, 1], came[t].at[right_y, pl.ds(8, 8)], left_y)

    def incoming(t, k):
        if k == 0:
            return out(t, 0, grad_ref.at[y, t], came[t].at[left_y, pl.ds(0, 16)], right_y)
        if k == 1:
            return out(t, 1, grad_ref.at[y, t], came[t].at[right_y, pl.ds(0, 16)], left_y)
        if k in (2, 3):
            return out(t, k, relay.at[t, k - 2], relay.at[t, k - 2], right_y)
        if k == 4:
            return out(t, 4, relay.at[t, 0], came[t].at[far_y, pl.ds(0, 8)], right_y)
        return out(t, 5, relay.at[t, 1], came[t].at[far_y, pl.ds(8, 8)], left_y)

    def post(t):
        for k in (2, 3, 0, 1):
            outgoing(t, k).start()
        came[t][y, pl.ds(0, 16)] = grad_ref[y, t]
        came[t][:, REFS] = jnp.zeros((NY, TOK, 128), BF16)

    def pass_on(t):
        for k in (2, 3):
            incoming(t, k).wait_recv()
            outgoing(t, k + 2).start()

    def block(dest):
        return pl.ds(8 * wrap(dest, NZ), 8)

    def ring(t, direction, h):
        buffers, target = (ring_up, up) if direction == 0 else (ring_down, down)
        count = hops(t)[direction]
        if h == 0:
            src = dense.at[t, block(z + count if direction == 0 else z - count + NZ)]
        else:
            src = buffers.at[t, h - 1]
        return remote(src, buffers.at[t, h], ring_s.at[t, direction, h], ring_r.at[t, direction, h], target, y, m)

    def add_up(t):
        for k in (0, 1, 4, 5):
            incoming(t, k).wait_recv()

        def body(s, carry):
            total = came[t][0, table_s[0, 8, s]].astype(F32)
            for o in range(1, NY):
                total += came[t][o, table_s[o, 8, s]].astype(F32)
            dense[t, s] = total.astype(BF16)
            return carry

        lax.fori_loop(0, 64, body, 0)
        ring(t, 0, 0).start()
        ring(t, 1, 0).start()

    def advance(t, h):
        for direction in (0, 1):
            count = hops(t)[direction]
            if h < count - 1:
                buffers = ring_up if direction == 0 else ring_down
                ring(t, direction, h).wait_recv()
                dest = z + (count - 1 - h) if direction == 0 else z - (count - 1 - h)
                buffers[t, h] = (buffers[t, h].astype(F32) + dense[t, block(dest)].astype(F32)).astype(BF16)
                ring(t, direction, h + 1).start()

    def near(t, k):
        if k == 2:
            source, target = (left_y, right_y) if t % 2 == 0 else (right_y, left_y)
        else:
            source, target = y, (right_y, left_y)[k]
        piece = rows.at[source, :, pl.ds(TOK * t, TOK)]
        return remote(piece, piece, near_s.at[t, k], near_r.at[t, k], z, target, m)

    def near_came(t, k):
        source = (left_y, right_y, far_y)[k]
        piece = rows.at[source, :, pl.ds(TOK * t, TOK)]
        return remote(piece, piece, near_s.at[t, k], near_r.at[t, k], z, right_y, m)

    def settle(t):
        counts = hops(t)
        ring(t, 0, counts[0] - 1).wait_recv()
        ring(t, 1, counts[1] - 1).wait_recv()
        total = (
            dense[t, block(z)].astype(F32)
            + ring_up[t, counts[0] - 1].astype(F32)
            + ring_down[t, counts[1] - 1].astype(F32)
        )
        rows[y, :, pl.ds(TOK * t, TOK)] = total.astype(BF16)
        near(t, 0).start()
        near(t, 1).start()

    def spread(t):
        near_came(t, t % 2).wait_recv()
        near(t, 2).start()

    events = []
    for t in range(CH):
        events.append((2 * t - 1, 0, functools.partial(post, t)))
        events.append((2 * t + 2, 1, functools.partial(pass_on, t)))
        events.append((2 * t + 4, 2, functools.partial(add_up, t)))
        for h in range(3):
            events.append((2 * t + h + 5, 3, functools.partial(advance, t, h)))
        events.append((2 * t + 8, 4, functools.partial(settle, t)))
        events.append((2 * t + 9, 5, functools.partial(spread, t)))
    for _, _, action in sorted(events, key=lambda event: event[:2]):
        action()
    for t in range(CH):
        near_came(t, 1 - t % 2).wait_recv()
        near_came(t, 2).wait_recv()

    row_grad = jnp.concatenate([rows[g].reshape(1024, 128) for g in range(4)], axis=1)

    def partial_of(dest):
        parts[wrap(dest, NZ)] = jnp.dot(normed_ref[wrap(dest, NZ)], row_grad, preferred_element_type=F32)

    def half(index):
        return slice(256 * index, 256 * index + 256)

    def sums(part, direction, h):
        buffers, firsts, target = (sum_up, first_up, up) if direction == 0 else (sum_down, first_down, down)
        src = firsts.at[part] if h == 0 else buffers.at[part, h - 1]
        return remote(src, buffers.at[part, h], sum_s.at[part, direction, h], sum_r.at[part, direction, h], target, y, m)

    def set_out(part, direction):
        count = hops(part)[direction]
        dest = z + count if direction == 0 else z - count
        (first_up if direction == 0 else first_down)[part] = parts[wrap(dest, NZ), :, half(part)].astype(BF16)
        sums(part, direction, 0).start()

    def hand_on(part, direction, h):
        count = hops(part)[direction]
        if h < count - 1:
            buffers = sum_up if direction == 0 else sum_down
            sums(part, direction, h).wait_recv()
            dest = z + (count - 1 - h) if direction == 0 else z - (count - 1 - h)
            buffers[part, h] = (buffers[part, h].astype(F32) + parts[wrap(dest, NZ), :, half(part)]).astype(BF16)
            sums(part, direction, h + 1).start()

    partial_of(z + 4)
    set_out(0, 0)
    set_out(1, 1)
    partial_of(z + 3)
    set_out(1, 0)
    partial_of(z - 3)
    set_out(0, 1)
    for h in range(3):
        if h < 2:
            partial_of(z + 2 - h)
            partial_of(z - 2 + h)
        else:
            partial_of(z)
        for part, direction in ((0, 0), (1, 1), (1, 0), (0, 1)):
            hand_on(part, direction, h)
    for part, ref in ((0, key_ref), (1, value_ref)):
        counts = hops(part)
        sums(part, 0, counts[0] - 1).wait_recv()
        sums(part, 1, counts[1] - 1).wait_recv()
        ref[...] = (
            parts[z, :, half(part)]
            + sum_up[part, counts[0] - 1].astype(F32)
            + sum_down[part, counts[1] - 1].astype(F32)
        )

    for t in range(CH):
        for k in range(6):
            outgoing(t, k).wait_send()
        for k in range(3):
            near(t, k).wait_send()
        for direction in (0, 1):
            for h in range(hops(t)[direction]):
                ring(t, direction, h).wait_send()
    for part in (0, 1):
        for direction in (0, 1):
            for h in range(hops(part)[direction]):
                sums(part, direction, h).wait_send()


def in_vmem(count):
    return [pl.BlockSpec(memory_space=VMEM)] * count


IN_SMEM = pl.BlockSpec(memory_space=pltpu.SMEM)


def dma(*shape):
    return pltpu.SemaphoreType.DMA(shape)


def talk(number):
    return pltpu.CompilerParams(collective_id=number, has_side_effects=True, vmem_limit_bytes=LIMIT)


def gather_features(store, gain):
    return pl.pallas_call(
        gather_kernel,
        out_shape=jax.ShapeDtypeStruct((NM, ROWS, 512), BF16),
        in_specs=in_vmem(2),
        out_specs=in_vmem(1)[0],
        scratch_shapes=[dma(11), dma(11)],
        compiler_params=talk(0),
        name="gather_features",
    )(store, gain)


def encode(everything, w_key, w_value):
    return pl.pallas_call(
        encode_kernel,
        out_shape=(jax.ShapeDtypeStruct((4, CH, 2, TOK, 128), BF16), jax.ShapeDtypeStruct((NY, 128, 256), BF16)),
        in_specs=in_vmem(3),
        out_specs=tuple(in_vmem(2)),
        compiler_params=pltpu.CompilerParams(vmem_limit_bytes=LIMIT),
        name="encode",
    )(everything, w_key, w_value)


def fetch_context(kv, turned, owner, store_row):
    return pl.pallas_call(
        context_kernel,
        out_shape=(
            jax.ShapeDtypeStruct((4, CH, REFS, TOK, 128), BF16),
            jax.ShapeDtypeStruct((NM, 128, 1024), BF16),
            jax.ShapeDtypeStruct((NY, 16, 128), I32),
        ),
        in_specs=in_vmem(4),
        out_specs=tuple(in_vmem(3)),
        scratch_shapes=[VMEM((64, TOK, 128), BF16)] * CH
        + [
            VMEM((CH, 3, REFS, TOK, 128), BF16),
            VMEM((CH, 2, 8, TOK, 128), BF16),
            pltpu.SMEM((NY, 16, 128), I32),
            dma(3, CH), dma(3, CH), dma(CH, 2, 4), dma(CH, 2, 4), dma(CH, 6), dma(CH, 6),
            dma(3), dma(3), dma(3), dma(3), dma(11), dma(11), dma(2),
        ],
        compiler_params=talk(1),
        name="fetch_context",
    )(kv, turned, owner, store_row)


def attention(table, queries, out_grad, context):
    return pl.pallas_call(
        attention_kernel,
        out_shape=(
            jax.ShapeDtypeStruct(queries.shape, BF16),
            jax.ShapeDtypeStruct(queries.shape, BF16),
            jax.ShapeDtypeStruct((4, CH, REFS, TOK, 128), BF16),
        ),
        in_specs=[IN_SMEM] + in_vmem(3),
        out_specs=tuple(in_vmem(3)),
        scratch_shapes=[VMEM((4, CH, REFS, TOK, 128), F32)],
        compiler_params=pltpu.CompilerParams(vmem_limit_bytes=LIMIT),
        name="attention",
    )(table, queries, out_grad, context)


def weight_grads(table, grads, normed):
    return pl.pallas_call(
        weight_kernel,
        out_shape=(jax.ShapeDtypeStruct((128, 256), F32), jax.ShapeDtypeStruct((128, 256), F32)),
        in_specs=[IN_SMEM] + in_vmem(2),
        out_specs=tuple(in_vmem(2)),
        scratch_shapes=[VMEM((NY, REFS + 1, TOK, 128), BF16)] * CH
        + [
            VMEM((CH, 2, 8, TOK, 128), BF16),
            VMEM((CH, 64, TOK, 128), BF16),
            VMEM((CH, 4, 8, TOK, 128), BF16),
            VMEM((CH, 4, 8, TOK, 128), BF16),
            VMEM((4, 8, 128, 128), BF16),
            VMEM((NZ, 128, 512), F32),
            VMEM((2, 128, 256), BF16),
            VMEM((2, 128, 256), BF16),
            VMEM((2, 4, 128, 256), BF16),
            VMEM((2, 4, 128, 256), BF16),
            dma(CH, 6), dma(CH, 6), dma(CH, 2, 4), dma(CH, 2, 4), dma(CH, 3), dma(CH, 3), dma(2, 2, 4), dma(2, 2, 4),
        ],
        compiler_params=talk(2),
        name="weight_grads",
    )(table, grads, normed)


def shards(queries, out_grad, owner, store_row, store, norm_gain, w_key, w_value):
    everything = gather_features(store.reshape(256, 512), norm_gain.reshape(1, 512))
    kv, turned = encode(everything, w_key, w_value)
    context, normed, table = fetch_context(kv, turned, owner, store_row)
    attended, query_grad, grads = attention(table, queries, out_grad, context)
    key_weight_grad, value_weight_grad = weight_grads(table, grads, normed)
    return (attended, query_grad, key_weight_grad, value_weight_grad)


def solution(mesh):
    in_specs = (
        P("dp", "mp"),
        P("dp", "mp"),
        P("dp", None),
        P("dp", None),
        P("dp", None, "mp"),
        P("mp"),
        P(None, "mp"),
        P(None, "mp"),
    )
    out_specs = (P("dp", "mp"), P("dp", "mp"), P("dp", "mp"), P("dp", "mp"))
    return jax.shard_map(shards, mesh=mesh, in_specs=in_specs, out_specs=out_specs, check_vma=False)
```

```python
import math

import jax
import jax.numpy as jnp
from jax import lax
from jax.experimental import pallas as pl
from jax.experimental.pallas import tpu as pltpu
from jax.sharding import PartitionSpec as P

MESH = pl.DeviceIdType.MESH
VMEM, SMEM = pltpu.VMEM, pltpu.SMEM
F32, BF16, I32 = jnp.float32, jnp.bfloat16, jnp.int32

HEAD = 128
ROOT = 1.0 / math.sqrt(HEAD)
EPS = 1e-06
NZ, NY, NM = 8, 4, 8
TOK = 32
REFS = 16
NONE = REFS
FLOOR = -3.0e38
DOWN = (((1,), (1,)), ((), ()))
ACROSS = (((0,), (0,)), ((), ()))
ORDER = (2, 1, 3)


def wrap(value, size):
    return lax.rem(value + size, size)


def place():
    d, m = lax.axis_index("dp"), lax.axis_index("mp")
    return lax.div(d, NY), lax.rem(d, NY), m


def remote(src, dst, send, recv, target):
    z, y, m = target
    return pltpu.make_async_remote_copy(
        src_ref=src, dst_ref=dst, send_sem=send, recv_sem=recv, device_id=(z * NY + y, m), device_id_type=MESH
    )


def greet(peers):
    barrier = pltpu.get_barrier_semaphore()
    for z, y, m in peers:
        pl.semaphore_signal(barrier, inc=1, device_id=(z * NY + y, m), device_id_type=MESH)
    return lambda: pl.semaphore_wait(barrier, len(peers))


class MpGather:
    def __init__(self, ref, low, high, send, recv):
        self.ref, self.send, self.recv = ref, send, recv
        self.z, self.y, self.m = place()
        self.right, self.left, self.opposite = wrap(self.m + 2, NM), wrap(self.m - 2, NM), wrap(self.m + 4, NM)
        self.twin = self.m + 1 - 2 * lax.rem(self.m, 2)
        self.low, self.high, self.whole = (0, low), (low, high - low), (0, high)

    def copy(self, block, part, target, k):
        piece = self.ref.at[block, pl.ds(*part)]
        return remote(piece, piece, self.send.at[k], self.recv.at[k], (self.z, self.y, target))

    def sent(self):
        m, left, right, opposite = self.m, self.left, self.right, self.opposite
        return [
            (m, self.low, right), (m, self.high, right), (m, self.high, left), (m, self.low, left), (m, self.whole, self.twin),
            (left, self.low, right), (right, self.high, left),
            (left, self.whole, self.twin), (right, self.whole, self.twin),
            (opposite, self.low, self.twin), (opposite, self.high, self.twin),
        ]

    def came(self):
        left, right, opposite, twin = self.left, self.right, self.opposite, self.twin
        tl, tr, to = wrap(twin - 2, NM), wrap(twin + 2, NM), wrap(twin + 4, NM)
        return [
            (left, self.low), (left, self.high), (right, self.high), (right, self.low), (twin, self.whole),
            (opposite, self.low), (opposite, self.high),
            (tl, self.whole), (tr, self.whole), (to, self.low), (to, self.high),
        ]

    def start(self, k):
        block, part, target = self.sent()[k]
        self.copy(block, part, target, k).start()

    def arrive(self, k):
        block, part = self.came()[k]
        self.copy(block, part, self.twin, k).wait_recv()

    def finish_send(self, k):
        block, part, target = self.sent()[k]
        self.copy(block, part, target, k).wait_send()

    def step(self, number):
        if number == 0:
            for k in (0, 2, 1, 3, 4):
                self.start(k)
        elif number == 1:
            self.arrive(0)
            self.start(5)
            self.arrive(2)
            self.start(6)
        elif number == 2:
            self.arrive(1)
            self.start(7)
            self.arrive(3)
            self.start(8)
        elif number == 3:
            self.arrive(5)
            self.start(9)
            self.arrive(6)
            self.start(10)
        else:
            for k in (4, 7, 8, 9, 10):
                self.arrive(k)
            for k in range(11):
                self.finish_send(k)


def counts(g):
    return (4, 3) if g % 2 == 0 else (3, 4)


def kernel(
    owner_s, row_s, q_hbm, o_hbm, store_hbm, gain_ref, key_hbm, value_hbm,
    att_ref, qg_ref, kw_ref, vw_ref,
    every, gains, w_key, w_value, table, table_s, qo, turned, normed, g0, g1, g2, g3,
    e_buf, pg_buf, stats, own_part, sent_part, came_part, f0, f1, f2, f3,
    dense, ring_up, ring_down, rows, parts, first_up, first_down, sum_up, sum_down,
    local, store_sems, gain_sems, tab_sems, qo_sems, every_s, every_r, turn_sems, normed_s, normed_r,
    ring_sems, stat_sems, back_sems, part_sems, row_sems, sum_sems,
):
    z, y, m = place()
    chunks, full = (g0, g1, g2, g3), (f0, f1, f2, f3)
    up, down = (wrap(z + 1, NZ), y, m), (wrap(z - 1, NZ), y, m)
    first_moves = MpGather(every, 4, 8, every_s, every_r)
    second_moves = MpGather(normed, 64, 128, normed_s, normed_r)

    def at_y(k):
        return wrap(y + k, NY)

    def from_y(k):
        return wrap(y - k, NY)

    def peer(k):
        return (z, at_y(k), m)

    met = greet(
        [peer(k) for k in (1, 2, 3)] + [up, down] + [(z, y, wrap(m + k, NM)) for k in range(1, NM)]
    )

    def at_home():
        quarter = pl.ds(pl.multiple_of(TOK * y, TOK), TOK)
        copies = [
            pltpu.make_async_copy(store_hbm.at[:, quarter], every.at[m, pl.ds(2 * y, 2)], local.at[0]),
            pltpu.make_async_copy(key_hbm, w_key, local.at[1]),
            pltpu.make_async_copy(value_hbm, w_value, local.at[2]),
        ]
        for h in range(2):
            for i, ref in enumerate((q_hbm, o_hbm)):
                copies.append(
                    pltpu.make_async_copy(ref.at[:, pl.ds(HEAD * h, HEAD)], qo.at[h, y, i], local.at[3 + 2 * h + i])
                )
        return copies

    home = at_home()
    for copy in home:
        copy.start()

    lane = lax.broadcasted_iota(I32, (8, 128), 1)
    line = lax.broadcasted_iota(I32, (8, 128), 0)
    ids = jnp.zeros((8, 128), I32)
    first = jnp.full((8, 128), NONE, I32)
    last = jnp.full((8, 128), -1, I32)
    for r in range(REFS):
        name = owner_s[r % 2, r // 2] * 2 + row_s[r % 2, r // 2]
        ids = jnp.where(lane == r, name, ids)
        first = jnp.where(lane == name, jnp.minimum(first, r), first)
        last = jnp.where(lane == name, r, last)
    second = jnp.where(last > first, last, NONE)
    table[y] = jnp.where(line == 0, ids, jnp.where(line == 1, first, second))
    gains[m] = jnp.broadcast_to(gain_ref[...].reshape(1, 512), (16, 512))
    for g in range(4):
        full[g][:, NONE] = jnp.zeros((NY, TOK, HEAD), F32)
    stats[:, y] = jnp.zeros((2, NY, 16, 128), F32)

    def store_copy(k, source, target):
        quarter = pl.ds(pl.multiple_of(TOK * target[1], TOK), TOK)
        return remote(
            store_hbm.at[:, quarter], every.at[m, pl.ds(2 * source, 2)], store_sems.at[0, k - 1], store_sems.at[1, k - 1], target
        )

    def gain_copy(k, source, target):
        return remote(gains.at[source], gains.at[source], gain_sems.at[0, k - 1], gain_sems.at[1, k - 1], (z, y, target))

    def tab_copy(k, source):
        return remote(table.at[source], table.at[source], tab_sems.at[0, k - 1], tab_sems.at[1, k - 1], peer(k))

    def qo_copy(h, i, k, source):
        ref = (q_hbm, o_hbm)[i]
        return remote(
            ref.at[:, pl.ds(HEAD * h, HEAD)], qo.at[h, source, i], qo_sems.at[0, h, i, k - 1], qo_sems.at[1, h, i, k - 1], peer(k)
        )

    met()
    for k in ORDER:
        store_copy(k, y, peer(k)).start()
    for k in range(1, NM):
        gain_copy(k, m, wrap(m + k, NM)).start()
    for k in ORDER:
        tab_copy(k, y).start()
    home[0].wait()
    for k in ORDER:
        store_copy(k, from_y(k), (z, y, m)).wait_recv()
    first_moves.step(0)
    for h in range(2):
        for k in ORDER:
            for i in range(2):
                qo_copy(h, i, k, y).start()
    for k in ORDER:
        tab_copy(k, from_y(k)).wait_recv()
    to_scalars = pltpu.make_async_copy(table, table_s, local.at[7])
    to_scalars.start()
    first_moves.step(1)
    first_moves.step(2)
    first_moves.step(3)
    first_moves.step(4)
    for k in range(1, NM):
        gain_copy(k, wrap(m - k, NM), m).wait_recv()
    home[1].wait()
    home[2].wait()

    total = jnp.zeros((256, 1), F32)
    for j in range(NM):
        part = every[j].reshape(256, 512).astype(F32)
        total += jnp.sum(part * part, axis=-1, keepdims=True)
    scale = lax.rsqrt(total * (1.0 / 4096.0) + EPS)
    for j in range(NM):
        gain = gains[j][0:1].astype(F32)
        block = every[j].reshape(256, 512).astype(F32) * scale * gain
        every[j] = block.astype(BF16).reshape(8, TOK, 512)

    def encode(h):
        encoded = jnp.zeros((256, 256), F32)
        for j in range(NM):
            depth, columns = slice(512 * j, 512 * (j + 1)), slice(HEAD * h, HEAD * (h + 1))
            weights = jnp.concatenate([w_key[depth, columns], w_value[depth, columns]], axis=1)
            encoded += jnp.dot(every[j].reshape(256, 512), weights, preferred_element_type=F32)
        for i in range(2):
            chunks[2 * h + i][pl.ds(8 * z, 8)] = encoded[:, HEAD * i : HEAD * (i + 1)].astype(BF16).reshape(8, TOK, HEAD)

    def ring_copy(g, direction, h, block):
        piece = chunks[g].at[pl.ds(8 * block, 8)]
        return remote(
            piece, piece, ring_sems.at[0, g, direction, h], ring_sems.at[1, g, direction, h], (up, down)[direction]
        )

    def ring_sent(g, direction, h):
        return ring_copy(g, direction, h, wrap(z - h, NZ) if direction == 0 else wrap(z + h, NZ))

    def ring_came(g, direction, h):
        return ring_copy(g, direction, h, wrap(z - 1 - h, NZ) if direction == 0 else wrap(z + 1 + h, NZ))

    def launch(g):
        for direction in (0, 1):
            ring_sent(g, direction, 0).start()

    def advance(g, h):
        for direction in (0, 1):
            if h < counts(g)[direction]:
                ring_came(g, direction, h).wait_recv()
                if h + 1 < counts(g)[direction]:
                    ring_sent(g, direction, h + 1).start()

    def turn_copy(k, source):
        lanes = pl.ds(pl.multiple_of(256 * source, 256), 256)
        return remote(
            turned.at[at_y(k)], normed.at[m, :, lanes], turn_sems.at[0, k - 1], turn_sems.at[1, k - 1], peer(k)
        )

    def turn():
        flat = every[m].reshape(256, 512).astype(F32).T.astype(BF16)
        for i in range(NY):
            turned[i] = flat[128 * i : 128 * (i + 1)]
        for k in ORDER:
            turn_copy(k, y).start()
        copy = pltpu.make_async_copy(turned.at[y], normed.at[m, :, pl.ds(pl.multiple_of(256 * y, 256), 256)], local.at[8])
        copy.start()
        copy.wait()

    context_span = lax.div(lax.broadcasted_iota(I32, (128, 128), 0), 64)
    query_span = lax.div(lax.broadcasted_iota(I32, (128, 128), 1), 64)
    same = context_span == query_span

    def context(g, b, p):
        picked = [chunks[g][table_s[b, 0, 4 * p + i]] for i in range(4)]
        return jnp.concatenate(picked, axis=0)

    def score(h, k):
        b = at_y(k)
        for p in range(4):
            queries, grads = qo[h, b, 0, 128 * p : 128 * (p + 1)], qo[h, b, 1, 128 * p : 128 * (p + 1)]
            scores = lax.dot_general(context(2 * h, b, p), queries, DOWN, preferred_element_type=F32) * ROOT
            scores = jnp.where(same, scores, FLOOR)
            prob_grad = lax.dot_general(context(2 * h + 1, b, p), grads, DOWN, preferred_element_type=F32)
            top = jnp.max(scores, axis=0, keepdims=True)
            weights = jnp.exp(scores - top)
            e_buf[h, k, p] = weights
            pg_buf[h, k, p] = prob_grad
            stats[h, y, b, p : p + 1] = top
            stats[h, y, b, 4 + p : 5 + p] = jnp.sum(weights, axis=0, keepdims=True)
            stats[h, y, b, 8 + p : 9 + p] = jnp.sum(weights * prob_grad, axis=0, keepdims=True)

    def stat_copy(h, k, source):
        piece = stats.at[h, source]
        return remote(piece, piece, stat_sems.at[0, h, k - 1], stat_sems.at[1, h, k - 1], peer(k))

    def part_copy(h, k):
        return remote(
            sent_part.at[h, k - 1], came_part.at[h, k - 1], part_sems.at[0, h, k - 1], part_sems.at[1, h, k - 1], peer(k)
        )

    def grads_of(h, k):
        b = at_y(k)
        tops = [stats[h, s, b, 0:4] for s in range(NY)]
        top = jnp.maximum(jnp.maximum(tops[0], tops[1]), jnp.maximum(tops[2], tops[3]))
        shares = [jnp.exp(each - top) for each in tops]
        whole, moment = jnp.zeros((4, 128), F32), jnp.zeros((4, 128), F32)
        for s in range(NY):
            whole += shares[s] * stats[h, s, b, 4:8]
            moment += shares[s] * stats[h, s, b, 8:12]
        factor = jnp.exp(stats[h, y, b, 0:4] - top) / whole
        delta = moment / whole
        for p in range(4):
            lines = slice(128 * p, 128 * (p + 1))
            queries, grads = qo[h, b, 0, lines], qo[h, b, 1, lines]
            keys, values = context(2 * h, b, p), context(2 * h + 1, b, p)
            probs = e_buf[h, k, p] * factor[p : p + 1]
            low = probs.astype(BF16)
            score_grad = (probs * (pg_buf[h, k, p] - delta[p : p + 1])).astype(BF16)
            attended = lax.dot_general(low, values, ACROSS, preferred_element_type=F32)
            query_grad = lax.dot_general(score_grad, keys, ACROSS, preferred_element_type=F32) * ROOT
            if k == 0:
                own_part[h, 0, lines] = attended
                own_part[h, 1, lines] = query_grad
            else:
                sent_part[h, k - 1, 0, lines] = attended.astype(BF16)
                sent_part[h, k - 1, 1, lines] = query_grad.astype(BF16)
            key_grad = jnp.dot(score_grad, queries, preferred_element_type=F32) * ROOT
            value_grad = jnp.dot(low, grads, preferred_element_type=F32)
            full[2 * h][b, 4 * p : 4 * p + 4] = key_grad.reshape(4, TOK, HEAD)
            full[2 * h + 1][b, 4 * p : 4 * p + 4] = value_grad.reshape(4, TOK, HEAD)
        if k > 0:
            part_copy(h, k).start()

    def outputs(h):
        for k in ORDER:
            part_copy(h, k).wait_recv()
        for i, ref in ((0, att_ref), (1, qg_ref)):
            whole = own_part[h, i]
            for k in ORDER:
                whole += came_part[h, k - 1, i].astype(F32)
            ref[:, HEAD * h : HEAD * (h + 1)] = whole.astype(BF16)

    def block(dest):
        return pl.ds(8 * wrap(dest, NZ), 8)

    def back_copy(g, direction, h):
        buffers, target = ((ring_up, up), (ring_down, down))[direction]
        count = counts(g)[direction]
        if h == 0:
            src = dense.at[g, block(z + count if direction == 0 else z - count)]
        else:
            src = buffers.at[g, h - 1]
        return remote(src, buffers.at[g, h], back_sems.at[0, g, direction, h], back_sems.at[1, g, direction, h], target)

    def add_up(g):
        def body(s, carry):
            whole = full[g][0, table_s[0, 1, s]] + full[g][0, table_s[0, 2, s]]
            for b in range(1, NY):
                whole += full[g][b, table_s[b, 1, s]] + full[g][b, table_s[b, 2, s]]
            dense[g, s] = whole.astype(BF16)
            return carry

        lax.fori_loop(0, 64, body, 0, unroll=4)
        for direction in (0, 1):
            back_copy(g, direction, 0).start()

    def pass_back(g, h):
        for direction in (0, 1):
            count = counts(g)[direction]
            if h < count - 1:
                buffers = (ring_up, ring_down)[direction]
                back_copy(g, direction, h).wait_recv()
                dest = z + (count - 1 - h) if direction == 0 else z - (count - 1 - h)
                buffers[g, h] = (buffers[g, h].astype(F32) + dense[g, block(dest)].astype(F32)).astype(BF16)
                back_copy(g, direction, h + 1).start()

    def row_copy(g, k, source):
        piece = rows.at[source, g]
        return remote(piece, piece, row_sems.at[0, g, k - 1], row_sems.at[1, g, k - 1], peer(k))

    def settle(g):
        n_up, n_down = counts(g)
        back_copy(g, 0, n_up - 1).wait_recv()
        back_copy(g, 1, n_down - 1).wait_recv()
        whole = dense[g, block(z)].astype(F32) + ring_up[g, n_up - 1].astype(F32) + ring_down[g, n_down - 1].astype(F32)
        rows[y, g] = whole.astype(BF16).reshape(256, HEAD)
        for k in ORDER:
            row_copy(g, k, y).start()

    def sum_copy(h, direction, n):
        buffers, firsts, target = ((sum_up, first_up, up), (sum_down, first_down, down))[direction]
        src = firsts.at[h] if n == 0 else buffers.at[h, n - 1]
        return remote(src, buffers.at[h, n], sum_sems.at[0, h, direction, n], sum_sems.at[1, h, direction, n], target)

    def weight_rows(h):
        for g in (2 * h, 2 * h + 1):
            for k in ORDER:
                row_copy(g, k, from_y(k)).wait_recv()
        return jnp.concatenate(
            [jnp.concatenate([rows[s, 2 * h], rows[s, 2 * h + 1]], axis=1) for s in range(NY)], axis=0
        )

    def weigh(h):
        row_grad = weight_rows(h)

        def partial_of(dest):
            return jnp.dot(normed[wrap(dest, NZ)], row_grad, preferred_element_type=F32)

        n_up, n_down = counts(h)
        if h == 0:
            first_up[h] = partial_of(z + n_up).astype(BF16)
            sum_copy(h, 0, 0).start()
            first_down[h] = partial_of(z - n_down).astype(BF16)
            sum_copy(h, 1, 0).start()
        else:
            first_down[h] = partial_of(z - n_down).astype(BF16)
            sum_copy(h, 1, 0).start()
            first_up[h] = partial_of(z + n_up).astype(BF16)
            sum_copy(h, 0, 0).start()
        for offset in (3, -3, 2, -2, 1, -1, 0):
            if offset not in (n_up, -n_down):
                parts[h, wrap(z + offset, NZ)] = partial_of(z + offset)

    def pass_sum(h, n):
        for direction in (h, 1 - h):
            count = counts(h)[direction]
            if n < count - 1:
                buffers = (sum_up, sum_down)[direction]
                sum_copy(h, direction, n).wait_recv()
                dest = z + (count - 1 - n) if direction == 0 else z - (count - 1 - n)
                buffers[h, n] = (buffers[h, n].astype(F32) + parts[h, wrap(dest, NZ)]).astype(BF16)
                sum_copy(h, direction, n + 1).start()

    def weights_out(h):
        n_up, n_down = counts(h)
        sum_copy(h, 0, n_up - 1).wait_recv()
        sum_copy(h, 1, n_down - 1).wait_recv()
        whole = parts[h, z] + sum_up[h, n_up - 1].astype(F32) + sum_down[h, n_down - 1].astype(F32)
        kw_ref[:, HEAD * h : HEAD * (h + 1)] = whole[:, 0:HEAD]
        vw_ref[:, HEAD * h : HEAD * (h + 1)] = whole[:, HEAD : 2 * HEAD]

    encode(0)
    launch(0)
    launch(1)
    encode(1)
    turn()
    advance(0, 0)
    advance(1, 0)
    launch(2)
    advance(0, 1)
    advance(1, 1)
    launch(3)
    advance(2, 0)
    for k in ORDER:
        turn_copy(k, from_y(k)).wait_recv()
    second_moves.step(0)
    advance(0, 2)
    advance(1, 2)
    advance(3, 0)
    advance(2, 1)
    advance(0, 3)
    advance(1, 3)
    advance(3, 1)
    second_moves.step(1)
    for copy in home[3:]:
        copy.wait()
    to_scalars.wait()
    for i in range(2):
        for k in ORDER:
            qo_copy(0, i, k, from_y(k)).wait_recv()
    score(0, 0)
    advance(2, 2)
    score(0, 1)
    advance(3, 2)
    score(0, 2)
    advance(2, 3)
    score(0, 3)
    for k in ORDER:
        stat_copy(0, k, y).start()
    advance(3, 3)
    second_moves.step(2)
    second_moves.step(3)
    for i in range(2):
        for k in ORDER:
            qo_copy(1, i, k, from_y(k)).wait_recv()
    for k in ORDER:
        stat_copy(0, k, from_y(k)).wait_recv()
    for k in (2, 1, 3, 0):
        grads_of(0, k)
    add_up(0)
    add_up(1)
    score(1, 0)
    score(1, 1)
    pass_back(0, 0)
    pass_back(1, 0)
    score(1, 2)
    score(1, 3)
    for k in ORDER:
        stat_copy(1, k, y).start()
    pass_back(0, 1)
    pass_back(1, 1)
    for k in ORDER:
        stat_copy(1, k, from_y(k)).wait_recv()
    grads_of(1, 2)
    pass_back(0, 2)
    pass_back(1, 2)
    grads_of(1, 1)
    grads_of(1, 3)
    settle(0)
    settle(1)
    grads_of(1, 0)
    add_up(2)
    add_up(3)
    second_moves.step(4)
    outputs(0)
    pass_back(2, 0)
    pass_back(3, 0)
    weigh(0)
    pass_back(2, 1)
    pass_back(3, 1)
    pass_sum(0, 0)
    pass_back(2, 2)
    pass_back(3, 2)
    pass_sum(0, 1)
    settle(2)
    settle(3)
    pass_sum(0, 2)
    outputs(1)
    weigh(1)
    weights_out(0)
    for n in range(3):
        pass_sum(1, n)
    weights_out(1)

    for k in ORDER:
        store_copy(k, y, peer(k)).wait_send()
        tab_copy(k, y).wait_send()
        turn_copy(k, y).wait_send()
        for h in range(2):
            for i in range(2):
                qo_copy(h, i, k, y).wait_send()
            stat_copy(h, k, y).wait_send()
            part_copy(h, k).wait_send()
        for g in range(4):
            row_copy(g, k, y).wait_send()
    for k in range(1, NM):
        gain_copy(k, m, wrap(m + k, NM)).wait_send()
    for direction in (0, 1):
        for g in range(4):
            for n in range(counts(g)[direction]):
                ring_sent(g, direction, n).wait_send()
                back_copy(g, direction, n).wait_send()
        for h in range(2):
            for n in range(counts(h)[direction]):
                sum_copy(h, direction, n).wait_send()


def dma(*shape):
    return pltpu.SemaphoreType.DMA(shape)


def shards(queries, out_grad, owner, store_row, store, norm_gain, w_key, w_value):
    in_smem, in_vmem, anywhere = (pl.BlockSpec(memory_space=space) for space in (SMEM, VMEM, pl.ANY))
    tile = (TOK, HEAD)
    return pl.pallas_call(
        kernel,
        out_shape=(
            jax.ShapeDtypeStruct((512, 256), BF16),
            jax.ShapeDtypeStruct((512, 256), BF16),
            jax.ShapeDtypeStruct((128, 256), F32),
            jax.ShapeDtypeStruct((128, 256), F32),
        ),
        in_specs=[in_smem, in_smem, anywhere, anywhere, anywhere, in_vmem, anywhere, anywhere],
        out_specs=(in_vmem,) * 4,
        scratch_shapes=[
            VMEM((NM, 8, TOK, 512), BF16),
            VMEM((NM, 16, 512), BF16),
            VMEM((4096, 256), BF16),
            VMEM((4096, 256), BF16),
            VMEM((NY, 8, 128), I32),
            SMEM((NY, 8, 128), I32),
            VMEM((2, NY, 2, 512, HEAD), BF16),
            VMEM((NY, 128, 256), BF16),
            VMEM((NM, 128, 1024), BF16),
        ]
        + [VMEM((64,) + tile, BF16)] * 4
        + [
            VMEM((2, NY, 4, 128, 128), F32),
            VMEM((2, NY, 4, 128, 128), F32),
            VMEM((2, NY, NY, 16, 128), F32),
            VMEM((2, 2, 512, HEAD), F32),
            VMEM((2, 3, 2, 512, HEAD), BF16),
            VMEM((2, 3, 2, 512, HEAD), BF16),
        ]
        + [VMEM((NY, REFS + 1) + tile, F32)] * 4
        + [
            VMEM((4, 64) + tile, BF16),
            VMEM((4, 4, 8) + tile, BF16),
            VMEM((4, 4, 8) + tile, BF16),
            VMEM((NY, 4, 256, HEAD), BF16),
            VMEM((2, NZ, 128, 256), F32),
            VMEM((2, 128, 256), BF16),
            VMEM((2, 128, 256), BF16),
            VMEM((2, 4, 128, 256), BF16),
            VMEM((2, 4, 128, 256), BF16),
            dma(9), dma(2, 3), dma(2, 7), dma(2, 3), dma(2, 2, 2, 3), dma(11), dma(11), dma(2, 3), dma(11), dma(11),
            dma(2, 4, 2, 4), dma(2, 2, 3), dma(2, 4, 2, 4), dma(2, 2, 3), dma(2, 4, 3), dma(2, 2, 2, 4),
        ],
        compiler_params=pltpu.CompilerParams(
            collective_id=0, has_side_effects=True, vmem_limit_bytes=60 * 1024 * 1024
        ),
        name="spans",
    )(owner.T, store_row.T, queries, out_grad, store, norm_gain, w_key, w_value)


def solution(mesh):
    in_specs = (
        P("dp", "mp"),
        P("dp", "mp"),
        P("dp", None),
        P("dp", None),
        P("dp", None, "mp"),
        P("mp"),
        P(None, "mp"),
        P(None, "mp"),
    )
    out_specs = (P("dp", "mp"), P("dp", "mp"), P("dp", "mp"), P("dp", "mp"))
    return jax.shard_map(shards, mesh=mesh, in_specs=in_specs, out_specs=out_specs, check_vma=False)
```

```python
import math

import jax
import jax.numpy as jnp
from jax import lax
from jax.experimental import pallas as pl
from jax.experimental.pallas import tpu as pltpu
from jax.sharding import PartitionSpec as P

MESH = pl.DeviceIdType.MESH
VMEM, SMEM = pltpu.VMEM, pltpu.SMEM
F32, BF16, I32 = jnp.float32, jnp.bfloat16, jnp.int32

HEAD = 128
ROOT = 1.0 / math.sqrt(HEAD)
EPS = 1e-06
NZ, NY, NM = 8, 4, 8
TOK = 32
REFS = 16
NONE = REFS
FLOOR = -3.0e38
DOWN = (((1,), (1,)), ((), ()))
ACROSS = (((0,), (0,)), ((), ()))
ORDER = (2, 1, 3)


def wrap(value, size):
    return lax.rem(value + size, size)


def place():
    d, m = lax.axis_index("dp"), lax.axis_index("mp")
    return lax.div(d, NY), lax.rem(d, NY), m


def remote(src, dst, send, recv, target):
    z, y, m = target
    return pltpu.make_async_remote_copy(
        src_ref=src, dst_ref=dst, send_sem=send, recv_sem=recv, device_id=(z * NY + y, m), device_id_type=MESH
    )


def greet(peers):
    barrier = pltpu.get_barrier_semaphore()
    for z, y, m in peers:
        pl.semaphore_signal(barrier, inc=1, device_id=(z * NY + y, m), device_id_type=MESH)
    return lambda: pl.semaphore_wait(barrier, len(peers))


class MpGather:
    def __init__(self, ref, base, size, send, recv, number):
        self.ref, self.send, self.recv, self.number = ref, send, recv, number
        self.z, self.y, self.m = place()
        self.right, self.left, self.opposite = wrap(self.m + 2, NM), wrap(self.m - 2, NM), wrap(self.m + 4, NM)
        self.twin = self.m + 1 - 2 * lax.rem(self.m, 2)
        self.low, self.high, self.whole = (base, size // 2), (base + size // 2, size // 2), (base, size)

    def copy(self, block, part, target, k):
        piece = self.ref.at[block, pl.ds(*part)]
        return remote(piece, piece, self.send.at[self.number, k], self.recv.at[self.number, k], (self.z, self.y, target))

    def sent(self):
        m, left, right, opposite = self.m, self.left, self.right, self.opposite
        return [
            (m, self.low, right), (m, self.high, right), (m, self.high, left), (m, self.low, left), (m, self.whole, self.twin),
            (left, self.low, right), (right, self.high, left),
            (left, self.whole, self.twin), (right, self.whole, self.twin),
            (opposite, self.low, self.twin), (opposite, self.high, self.twin),
        ]

    def came(self):
        left, right, opposite, twin = self.left, self.right, self.opposite, self.twin
        tl, tr, to = wrap(twin - 2, NM), wrap(twin + 2, NM), wrap(twin + 4, NM)
        return [
            (left, self.low), (left, self.high), (right, self.high), (right, self.low), (twin, self.whole),
            (opposite, self.low), (opposite, self.high),
            (tl, self.whole), (tr, self.whole), (to, self.low), (to, self.high),
        ]

    def start(self, k):
        block, part, target = self.sent()[k]
        self.copy(block, part, target, k).start()

    def arrive(self, k):
        block, part = self.came()[k]
        self.copy(block, part, self.twin, k).wait_recv()

    def finish_send(self, k):
        block, part, target = self.sent()[k]
        self.copy(block, part, target, k).wait_send()

    def step(self, number):
        if number == 0:
            for k in (0, 2, 1, 3, 4):
                self.start(k)
        elif number == 1:
            self.arrive(0)
            self.start(5)
            self.arrive(2)
            self.start(6)
        elif number == 2:
            self.arrive(1)
            self.start(7)
            self.arrive(3)
            self.start(8)
        elif number == 3:
            self.arrive(5)
            self.start(9)
            self.arrive(6)
            self.start(10)
        else:
            for k in (4, 7, 8, 9, 10):
                self.arrive(k)
            for k in range(11):
                self.finish_send(k)


def counts(g):
    return (4, 3) if g % 2 == 0 else (3, 4)


def kernel(
    owner_s, row_s, q_hbm, o_hbm, store_hbm, gain_ref, key_hbm, value_hbm,
    att_ref, qg_ref, kw_ref, vw_ref,
    every, gains, w_key, w_value, table, table_s, qo, turned, normed, g0, g1, g2, g3,
    e_buf, pg_buf, stats, own_part, sent_part, came_part, f0, f1, f2, f3,
    dense, ring_up, ring_down, rows, parts, first_up, first_down, sum_up, sum_down,
    local, store_sems, gain_sems, tab_sems, qo_sems, every_s, every_r, turn_sems, normed_s, normed_r,
    ring_sems, stat_sems, back_sems, part_sems, row_sems, sum_sems,
):
    z, y, m = place()
    chunks, full = (g0, g1, g2, g3), (f0, f1, f2, f3)
    up, down = (wrap(z + 1, NZ), y, m), (wrap(z - 1, NZ), y, m)

    def at_y(k):
        return wrap(y + k, NY)

    def from_y(k):
        return wrap(y - k, NY)

    def peer(k):
        return (z, at_y(k), m)

    pieces = [MpGather(every, 2 * from_y(k), 2, every_s, every_r, k) for k in range(NY)]
    second_moves = MpGather(normed, 0, 128, normed_s, normed_r, 0)

    met = greet(
        [peer(k) for k in (1, 2, 3)] + [up, down] + [(z, y, wrap(m + k, NM)) for k in range(1, NM)]
    )

    def at_home():
        quarter = pl.ds(pl.multiple_of(TOK * y, TOK), TOK)
        copies = [
            pltpu.make_async_copy(store_hbm.at[:, quarter], every.at[m, pl.ds(2 * y, 2)], local.at[0]),
            pltpu.make_async_copy(key_hbm, w_key, local.at[1]),
            pltpu.make_async_copy(value_hbm, w_value, local.at[2]),
        ]
        for h in range(2):
            for i, ref in enumerate((q_hbm, o_hbm)):
                copies.append(
                    pltpu.make_async_copy(ref.at[:, pl.ds(HEAD * h, HEAD)], qo.at[h, y, i], local.at[3 + 2 * h + i])
                )
        return copies

    home = at_home()
    for copy in home:
        copy.start()

    lane = lax.broadcasted_iota(I32, (8, 128), 1)
    line = lax.broadcasted_iota(I32, (8, 128), 0)
    ids = jnp.zeros((8, 128), I32)
    first = jnp.full((8, 128), NONE, I32)
    last = jnp.full((8, 128), -1, I32)
    for r in range(REFS):
        name = owner_s[r % 2, r // 2] * 2 + row_s[r % 2, r // 2]
        ids = jnp.where(lane == r, name, ids)
        first = jnp.where(lane == name, jnp.minimum(first, r), first)
        last = jnp.where(lane == name, r, last)
    second = jnp.where(last > first, last, NONE)
    table[y] = jnp.where(line == 0, ids, jnp.where(line == 1, first, second))
    gains[m] = jnp.broadcast_to(gain_ref[...].reshape(1, 512), (16, 512))
    for g in range(4):
        full[g][:, NONE] = jnp.zeros((NY, TOK, HEAD), F32)
    stats[:, y] = jnp.zeros((2, NY, 16, 128), F32)

    def store_copy(k, source, target):
        quarter = pl.ds(pl.multiple_of(TOK * target[1], TOK), TOK)
        return remote(
            store_hbm.at[:, quarter], every.at[m, pl.ds(2 * source, 2)], store_sems.at[0, k - 1], store_sems.at[1, k - 1], target
        )

    def gain_copy(k, source, target):
        return remote(gains.at[source], gains.at[source], gain_sems.at[0, k - 1], gain_sems.at[1, k - 1], (z, y, target))

    def tab_copy(k, source):
        return remote(table.at[source], table.at[source], tab_sems.at[0, k - 1], tab_sems.at[1, k - 1], peer(k))

    def qo_copy(h, i, k, source):
        ref = (q_hbm, o_hbm)[i]
        return remote(
            ref.at[:, pl.ds(HEAD * h, HEAD)], qo.at[h, source, i], qo_sems.at[0, h, i, k - 1], qo_sems.at[1, h, i, k - 1], peer(k)
        )

    met()
    for k in ORDER:
        store_copy(k, y, peer(k)).start()
    for k in range(1, NM):
        gain_copy(k, m, wrap(m + k, NM)).start()
    for k in ORDER:
        tab_copy(k, y).start()
    home[0].wait()
    pieces[0].step(0)
    for k in (1, 3):
        store_copy(k, from_y(k), (z, y, m)).wait_recv()
        pieces[k].step(0)
    pieces[0].step(1)
    store_copy(2, from_y(2), (z, y, m)).wait_recv()
    pieces[2].step(0)
    for h in range(2):
        for k in ORDER:
            for i in range(2):
                qo_copy(h, i, k, y).start()
    for k in ORDER:
        tab_copy(k, from_y(k)).wait_recv()
    to_scalars = pltpu.make_async_copy(table, table_s, local.at[7])
    to_scalars.start()
    pieces[1].step(1)
    pieces[0].step(2)
    pieces[3].step(1)
    pieces[0].step(3)
    pieces[1].step(2)
    pieces[2].step(1)
    pieces[3].step(2)
    pieces[1].step(3)
    pieces[2].step(2)
    pieces[3].step(3)
    pieces[2].step(3)
    for k in (0, 1, 3, 2):
        pieces[k].step(4)
    for k in range(1, NM):
        gain_copy(k, wrap(m - k, NM), m).wait_recv()
    home[1].wait()
    home[2].wait()

    total = jnp.zeros((256, 1), F32)
    for j in range(NM):
        part = every[j].reshape(256, 512).astype(F32)
        total += jnp.sum(part * part, axis=-1, keepdims=True)
    scale = lax.rsqrt(total * (1.0 / 4096.0) + EPS)
    for j in range(NM):
        gain = gains[j][0:1].astype(F32)
        block = every[j].reshape(256, 512).astype(F32) * scale * gain
        every[j] = block.astype(BF16).reshape(8, TOK, 512)

    def encode(h):
        encoded = jnp.zeros((256, 256), F32)
        for j in range(NM):
            depth, columns = slice(512 * j, 512 * (j + 1)), slice(HEAD * h, HEAD * (h + 1))
            weights = jnp.concatenate([w_key[depth, columns], w_value[depth, columns]], axis=1)
            encoded += jnp.dot(every[j].reshape(256, 512), weights, preferred_element_type=F32)
        for i in range(2):
            chunks[2 * h + i][pl.ds(8 * z, 8)] = encoded[:, HEAD * i : HEAD * (i + 1)].astype(BF16).reshape(8, TOK, HEAD)

    def ring_copy(g, direction, h, block):
        piece = chunks[g].at[pl.ds(8 * block, 8)]
        return remote(
            piece, piece, ring_sems.at[0, g, direction, h], ring_sems.at[1, g, direction, h], (up, down)[direction]
        )

    def ring_sent(g, direction, h):
        return ring_copy(g, direction, h, wrap(z - h, NZ) if direction == 0 else wrap(z + h, NZ))

    def ring_came(g, direction, h):
        return ring_copy(g, direction, h, wrap(z - 1 - h, NZ) if direction == 0 else wrap(z + 1 + h, NZ))

    def launch(g):
        for direction in (0, 1):
            ring_sent(g, direction, 0).start()

    def advance(g, h):
        for direction in (0, 1):
            if h < counts(g)[direction]:
                ring_came(g, direction, h).wait_recv()
                if h + 1 < counts(g)[direction]:
                    ring_sent(g, direction, h + 1).start()

    def turn_copy(k, source):
        lanes = pl.ds(pl.multiple_of(256 * source, 256), 256)
        return remote(
            turned.at[at_y(k)], normed.at[m, :, lanes], turn_sems.at[0, k - 1], turn_sems.at[1, k - 1], peer(k)
        )

    def turn():
        flat = every[m].reshape(256, 512).astype(F32).T.astype(BF16)
        for i in range(NY):
            turned[i] = flat[128 * i : 128 * (i + 1)]
        for k in ORDER:
            turn_copy(k, y).start()
        copy = pltpu.make_async_copy(turned.at[y], normed.at[m, :, pl.ds(pl.multiple_of(256 * y, 256), 256)], local.at[8])
        copy.start()
        copy.wait()

    context_span = lax.div(lax.broadcasted_iota(I32, (128, 128), 0), 64)
    query_span = lax.div(lax.broadcasted_iota(I32, (128, 128), 1), 64)
    same = context_span == query_span

    def context(g, b, p):
        picked = [chunks[g][table_s[b, 0, 4 * p + i]] for i in range(4)]
        return jnp.concatenate(picked, axis=0)

    def score(h, k):
        b = at_y(k)
        for p in range(4):
            queries, grads = qo[h, b, 0, 128 * p : 128 * (p + 1)], qo[h, b, 1, 128 * p : 128 * (p + 1)]
            scores = lax.dot_general(context(2 * h, b, p), queries, DOWN, preferred_element_type=F32) * ROOT
            scores = jnp.where(same, scores, FLOOR)
            prob_grad = lax.dot_general(context(2 * h + 1, b, p), grads, DOWN, preferred_element_type=F32)
            top = jnp.max(scores, axis=0, keepdims=True)
            weights = jnp.exp(scores - top)
            e_buf[h, k, p] = weights
            pg_buf[h, k, p] = prob_grad
            stats[h, y, b, p : p + 1] = top
            stats[h, y, b, 4 + p : 5 + p] = jnp.sum(weights, axis=0, keepdims=True)
            stats[h, y, b, 8 + p : 9 + p] = jnp.sum(weights * prob_grad, axis=0, keepdims=True)

    def stat_copy(h, k, source):
        piece = stats.at[h, source]
        return remote(piece, piece, stat_sems.at[0, h, k - 1], stat_sems.at[1, h, k - 1], peer(k))

    def part_copy(h, k):
        return remote(
            sent_part.at[h, k - 1], came_part.at[h, k - 1], part_sems.at[0, h, k - 1], part_sems.at[1, h, k - 1], peer(k)
        )

    def grads_of(h, k):
        b = at_y(k)
        tops = [stats[h, s, b, 0:4] for s in range(NY)]
        top = jnp.maximum(jnp.maximum(tops[0], tops[1]), jnp.maximum(tops[2], tops[3]))
        shares = [jnp.exp(each - top) for each in tops]
        whole, moment = jnp.zeros((4, 128), F32), jnp.zeros((4, 128), F32)
        for s in range(NY):
            whole += shares[s] * stats[h, s, b, 4:8]
            moment += shares[s] * stats[h, s, b, 8:12]
        factor = jnp.exp(stats[h, y, b, 0:4] - top) / whole
        delta = moment / whole
        for p in range(4):
            lines = slice(128 * p, 128 * (p + 1))
            queries, grads = qo[h, b, 0, lines], qo[h, b, 1, lines]
            keys, values = context(2 * h, b, p), context(2 * h + 1, b, p)
            probs = e_buf[h, k, p] * factor[p : p + 1]
            low = probs.astype(BF16)
            score_grad = (probs * (pg_buf[h, k, p] - delta[p : p + 1])).astype(BF16)
            attended = lax.dot_general(low, values, ACROSS, preferred_element_type=F32)
            query_grad = lax.dot_general(score_grad, keys, ACROSS, preferred_element_type=F32) * ROOT
            if k == 0:
                own_part[h, 0, lines] = attended
                own_part[h, 1, lines] = query_grad
            else:
                sent_part[h, k - 1, 0, lines] = attended.astype(BF16)
                sent_part[h, k - 1, 1, lines] = query_grad.astype(BF16)
            key_grad = jnp.dot(score_grad, queries, preferred_element_type=F32) * ROOT
            value_grad = jnp.dot(low, grads, preferred_element_type=F32)
            full[2 * h][b, 4 * p : 4 * p + 4] = key_grad.reshape(4, TOK, HEAD)
            full[2 * h + 1][b, 4 * p : 4 * p + 4] = value_grad.reshape(4, TOK, HEAD)
        if k > 0:
            part_copy(h, k).start()

    def outputs(h):
        for k in ORDER:
            part_copy(h, k).wait_recv()
        for i, ref in ((0, att_ref), (1, qg_ref)):
            whole = own_part[h, i]
            for k in ORDER:
                whole += came_part[h, k - 1, i].astype(F32)
            ref[:, HEAD * h : HEAD * (h + 1)] = whole.astype(BF16)

    def block(dest):
        return pl.ds(8 * wrap(dest, NZ), 8)

    def back_copy(g, direction, h):
        buffers, target = ((ring_up, up), (ring_down, down))[direction]
        count = counts(g)[direction]
        if h == 0:
            src = dense.at[g, block(z + count if direction == 0 else z - count)]
        else:
            src = buffers.at[g, h - 1]
        return remote(src, buffers.at[g, h], back_sems.at[0, g, direction, h], back_sems.at[1, g, direction, h], target)

    def add_up(g):
        def body(s, carry):
            whole = full[g][0, table_s[0, 1, s]] + full[g][0, table_s[0, 2, s]]
            for b in range(1, NY):
                whole += full[g][b, table_s[b, 1, s]] + full[g][b, table_s[b, 2, s]]
            dense[g, s] = whole.astype(BF16)
            return carry

        lax.fori_loop(0, 64, body, 0, unroll=4)
        for direction in (0, 1):
            back_copy(g, direction, 0).start()

    def pass_back(g, h):
        for direction in (0, 1):
            count = counts(g)[direction]
            if h < count - 1:
                buffers = (ring_up, ring_down)[direction]
                back_copy(g, direction, h).wait_recv()
                dest = z + (count - 1 - h) if direction == 0 else z - (count - 1 - h)
                buffers[g, h] = (buffers[g, h].astype(F32) + dense[g, block(dest)].astype(F32)).astype(BF16)
                back_copy(g, direction, h + 1).start()

    def row_copy(g, k, source):
        piece = rows.at[source, g]
        return remote(piece, piece, row_sems.at[0, g, k - 1], row_sems.at[1, g, k - 1], peer(k))

    def settle(g):
        n_up, n_down = counts(g)
        back_copy(g, 0, n_up - 1).wait_recv()
        back_copy(g, 1, n_down - 1).wait_recv()
        whole = dense[g, block(z)].astype(F32) + ring_up[g, n_up - 1].astype(F32) + ring_down[g, n_down - 1].astype(F32)
        rows[y, g] = whole.astype(BF16).reshape(256, HEAD)
        for k in ORDER:
            row_copy(g, k, y).start()

    def sum_copy(g, direction, n):
        buffers, firsts, target = ((sum_up, first_up, up), (sum_down, first_down, down))[direction]
        src = firsts.at[g] if n == 0 else buffers.at[g, n - 1]
        return remote(src, buffers.at[g, n], sum_sems.at[0, g, direction, n], sum_sems.at[1, g, direction, n], target)

    def weigh(g):
        for k in ORDER:
            row_copy(g, k, from_y(k)).wait_recv()
        row_grad = jnp.concatenate([rows[s, g] for s in range(NY)], axis=0)

        def partial_of(dest):
            return jnp.dot(normed[wrap(dest, NZ)], row_grad, preferred_element_type=F32)

        n_up, n_down = counts(g)
        for direction in (g % 2, 1 - g % 2):
            if direction == 0:
                first_up[g] = partial_of(z + n_up).astype(BF16)
            else:
                first_down[g] = partial_of(z - n_down).astype(BF16)
            sum_copy(g, direction, 0).start()
        for offset in (3, -3, 2, -2, 1, -1, 0):
            if offset not in (n_up, -n_down):
                parts[g, wrap(z + offset, NZ)] = partial_of(z + offset)

    def pass_sum(g, n):
        for direction in (g % 2, 1 - g % 2):
            count = counts(g)[direction]
            if n < count - 1:
                buffers = (sum_up, sum_down)[direction]
                sum_copy(g, direction, n).wait_recv()
                dest = z + (count - 1 - n) if direction == 0 else z - (count - 1 - n)
                buffers[g, n] = (buffers[g, n].astype(F32) + parts[g, wrap(dest, NZ)]).astype(BF16)
                sum_copy(g, direction, n + 1).start()

    def weights_out(g):
        n_up, n_down = counts(g)
        sum_copy(g, 0, n_up - 1).wait_recv()
        sum_copy(g, 1, n_down - 1).wait_recv()
        whole = parts[g, z] + sum_up[g, n_up - 1].astype(F32) + sum_down[g, n_down - 1].astype(F32)
        ref, first_column = (kw_ref, vw_ref)[g % 2], HEAD * (g // 2)
        ref[:, first_column : first_column + HEAD] = whole

    encode(0)
    launch(0)
    launch(1)
    encode(1)
    turn()
    advance(0, 0)
    advance(1, 0)
    launch(2)
    advance(0, 1)
    advance(1, 1)
    launch(3)
    advance(2, 0)
    for k in ORDER:
        turn_copy(k, from_y(k)).wait_recv()
    second_moves.step(0)
    advance(0, 2)
    advance(1, 2)
    advance(3, 0)
    advance(2, 1)
    advance(0, 3)
    advance(1, 3)
    advance(3, 1)
    for copy in home[3:]:
        copy.wait()
    to_scalars.wait()
    for i in range(2):
        for k in ORDER:
            qo_copy(0, i, k, from_y(k)).wait_recv()
    score(0, 0)
    advance(2, 2)
    score(0, 1)
    advance(3, 2)
    score(0, 2)
    score(0, 3)
    for k in ORDER:
        stat_copy(0, k, y).start()
    advance(2, 3)
    advance(3, 3)
    for i in range(2):
        for k in ORDER:
            qo_copy(1, i, k, from_y(k)).wait_recv()
    for k in range(NY):
        score(1, k)
    for k in ORDER:
        stat_copy(1, k, y).start()
    for k in ORDER:
        stat_copy(0, k, from_y(k)).wait_recv()
    for k in (2, 1, 3, 0):
        grads_of(0, k)
    add_up(0)
    add_up(1)
    second_moves.step(1)
    for k in ORDER:
        stat_copy(1, k, from_y(k)).wait_recv()
    grads_of(1, 2)
    grads_of(1, 1)
    pass_back(0, 0)
    pass_back(1, 0)
    grads_of(1, 3)
    grads_of(1, 0)
    pass_back(0, 1)
    pass_back(1, 1)
    add_up(2)
    add_up(3)
    second_moves.step(2)
    second_moves.step(3)
    pass_back(0, 2)
    pass_back(1, 2)
    pass_back(2, 0)
    pass_back(3, 0)
    settle(0)
    settle(1)
    second_moves.step(4)
    pass_back(2, 1)
    pass_back(3, 1)
    weigh(0)
    weigh(1)
    pass_back(2, 2)
    pass_back(3, 2)
    pass_sum(0, 0)
    pass_sum(1, 0)
    settle(2)
    settle(3)
    pass_sum(0, 1)
    pass_sum(1, 1)
    outputs(0)
    outputs(1)
    weigh(2)
    weigh(3)
    pass_sum(0, 2)
    pass_sum(1, 2)
    pass_sum(2, 0)
    pass_sum(3, 0)
    weights_out(0)
    weights_out(1)
    pass_sum(2, 1)
    pass_sum(3, 1)
    pass_sum(2, 2)
    pass_sum(3, 2)
    weights_out(2)
    weights_out(3)

    for k in ORDER:
        store_copy(k, y, peer(k)).wait_send()
        tab_copy(k, y).wait_send()
        turn_copy(k, y).wait_send()
        for h in range(2):
            for i in range(2):
                qo_copy(h, i, k, y).wait_send()
            stat_copy(h, k, y).wait_send()
            part_copy(h, k).wait_send()
        for g in range(4):
            row_copy(g, k, y).wait_send()
    for k in range(1, NM):
        gain_copy(k, m, wrap(m + k, NM)).wait_send()
    for direction in (0, 1):
        for g in range(4):
            for n in range(counts(g)[direction]):
                ring_sent(g, direction, n).wait_send()
                back_copy(g, direction, n).wait_send()
                sum_copy(g, direction, n).wait_send()


def hand_over(*refs):
    for source, target in zip(refs[:4], refs[4:]):
        target[...] = source[...]


def dma(*shape):
    return pltpu.SemaphoreType.DMA(shape)


def shards(queries, out_grad, owner, store_row, store, norm_gain, w_key, w_value):
    in_smem, in_vmem, anywhere = (pl.BlockSpec(memory_space=space) for space in (SMEM, VMEM, pl.ANY))
    tile = (TOK, HEAD)
    results = pl.pallas_call(
        kernel,
        out_shape=(
            jax.ShapeDtypeStruct((512, 256), BF16),
            jax.ShapeDtypeStruct((512, 256), BF16),
            jax.ShapeDtypeStruct((128, 256), F32),
            jax.ShapeDtypeStruct((128, 256), F32),
        ),
        in_specs=[in_smem, in_smem, anywhere, anywhere, anywhere, in_vmem, anywhere, anywhere],
        out_specs=(in_vmem,) * 4,
        scratch_shapes=[
            VMEM((NM, 8, TOK, 512), BF16),
            VMEM((NM, 16, 512), BF16),
            VMEM((4096, 256), BF16),
            VMEM((4096, 256), BF16),
            VMEM((NY, 8, 128), I32),
            SMEM((NY, 8, 128), I32),
            VMEM((2, NY, 2, 512, HEAD), BF16),
            VMEM((NY, 128, 256), BF16),
            VMEM((NM, 128, 1024), BF16),
        ]
        + [VMEM((64,) + tile, BF16)] * 4
        + [
            VMEM((2, NY, 4, 128, 128), F32),
            VMEM((2, NY, 4, 128, 128), F32),
            VMEM((2, NY, NY, 16, 128), F32),
            VMEM((2, 2, 512, HEAD), F32),
            VMEM((2, 3, 2, 512, HEAD), BF16),
            VMEM((2, 3, 2, 512, HEAD), BF16),
        ]
        + [VMEM((NY, REFS + 1) + tile, F32)] * 4
        + [
            VMEM((4, 64) + tile, BF16),
            VMEM((4, 4, 8) + tile, BF16),
            VMEM((4, 4, 8) + tile, BF16),
            VMEM((NY, 4, 256, HEAD), BF16),
            VMEM((4, NZ, 128, HEAD), F32),
            VMEM((4, 128, HEAD), BF16),
            VMEM((4, 128, HEAD), BF16),
            VMEM((4, 4, 128, HEAD), BF16),
            VMEM((4, 4, 128, HEAD), BF16),
            dma(9), dma(2, 3), dma(2, 7), dma(2, 3), dma(2, 2, 2, 3), dma(4, 11), dma(4, 11), dma(2, 3), dma(1, 11), dma(1, 11),
            dma(2, 4, 2, 4), dma(2, 2, 3), dma(2, 4, 2, 4), dma(2, 2, 3), dma(2, 4, 3), dma(2, 4, 2, 4),
        ],
        compiler_params=pltpu.CompilerParams(
            collective_id=0, has_side_effects=True, vmem_limit_bytes=60 * 1024 * 1024
        ),
        name="spans",
    )(owner.T, store_row.T, queries, out_grad, store, norm_gain, w_key, w_value)
    return pl.pallas_call(
        hand_over,
        out_shape=tuple(jax.ShapeDtypeStruct(each.shape, each.dtype) for each in results),
        in_specs=[in_vmem] * 4,
        out_specs=(in_vmem,) * 4,
        name="hand_over",
    )(*results)


def solution(mesh):
    in_specs = (
        P("dp", "mp"),
        P("dp", "mp"),
        P("dp", None),
        P("dp", None),
        P("dp", None, "mp"),
        P("mp"),
        P(None, "mp"),
        P(None, "mp"),
    )
    out_specs = (P("dp", "mp"), P("dp", "mp"), P("dp", "mp"), P("dp", "mp"))
    return jax.shard_map(shards, mesh=mesh, in_specs=in_specs, out_specs=out_specs, check_vma=False)
```

```python
import functools
import math

import jax
import jax.numpy as jnp
from jax import lax
from jax.experimental import pallas as pl
from jax.experimental.pallas import tpu as pltpu
from jax.sharding import PartitionSpec as P

MESH = pl.DeviceIdType.MESH
VMEM, SMEM = pltpu.VMEM, pltpu.SMEM
F32, BF16, I32 = jnp.float32, jnp.bfloat16, jnp.int32

HEAD = 128
ROOT = 1.0 / math.sqrt(HEAD)
EPS = 1e-06
NZ, NY, NM = 8, 4, 8
TOK = 32
REFS = 16
NONE = REFS
FLOOR = -3.0e38
DOWN = (((1,), (1,)), ((), ()))
ACROSS = (((0,), (0,)), ((), ()))
ORDER = (1, 3, 2)


def wrap(value, size):
    return lax.rem(value + size, size)


def place():
    d, m = lax.axis_index("dp"), lax.axis_index("mp")
    return lax.div(d, NY), lax.rem(d, NY), m


def remote(src, dst, send, recv, target):
    z, y, m = target
    return pltpu.make_async_remote_copy(
        src_ref=src, dst_ref=dst, send_sem=send, recv_sem=recv, device_id=(z * NY + y, m), device_id_type=MESH
    )


def greet(peers):
    barrier = pltpu.get_barrier_semaphore()
    for z, y, m in peers:
        pl.semaphore_signal(barrier, inc=1, device_id=(z * NY + y, m), device_id_type=MESH)
    return lambda: pl.semaphore_wait(barrier, len(peers))


class MpGather:
    def __init__(self, ref, base, size, send, recv, number):
        self.ref, self.send, self.recv, self.number = ref, send, recv, number
        self.z, self.y, self.m = place()
        self.right, self.left, self.opposite = wrap(self.m + 2, NM), wrap(self.m - 2, NM), wrap(self.m + 4, NM)
        self.twin = self.m + 1 - 2 * lax.rem(self.m, 2)
        self.low, self.high, self.whole = (base, size // 2), (base + size // 2, size // 2), (base, size)

    def copy(self, block, part, target, k):
        piece = self.ref.at[block, pl.ds(*part)]
        return remote(piece, piece, self.send.at[self.number, k], self.recv.at[self.number, k], (self.z, self.y, target))

    def sent(self):
        m, left, right, opposite = self.m, self.left, self.right, self.opposite
        return [
            (m, self.low, right), (m, self.high, right), (m, self.high, left), (m, self.low, left), (m, self.whole, self.twin),
            (left, self.low, right), (right, self.high, left),
            (left, self.whole, self.twin), (right, self.whole, self.twin),
            (opposite, self.low, self.twin), (opposite, self.high, self.twin),
        ]

    def came(self):
        left, right, opposite, twin = self.left, self.right, self.opposite, self.twin
        tl, tr, to = wrap(twin - 2, NM), wrap(twin + 2, NM), wrap(twin + 4, NM)
        return [
            (left, self.low), (left, self.high), (right, self.high), (right, self.low), (twin, self.whole),
            (opposite, self.low), (opposite, self.high),
            (tl, self.whole), (tr, self.whole), (to, self.low), (to, self.high),
        ]

    def start(self, k):
        block, part, target = self.sent()[k]
        self.copy(block, part, target, k).start()

    def arrive(self, k):
        block, part = self.came()[k]
        self.copy(block, part, self.twin, k).wait_recv()

    def finish_send(self, k):
        block, part, target = self.sent()[k]
        self.copy(block, part, target, k).wait_send()

    def step(self, number):
        if number == 0:
            for k in (0, 2, 1, 3, 4):
                self.start(k)
        elif number == 1:
            self.arrive(0)
            self.start(5)
            self.arrive(2)
            self.start(6)
        elif number == 2:
            self.arrive(1)
            self.start(7)
            self.arrive(3)
            self.start(8)
        elif number == 3:
            self.arrive(5)
            self.start(9)
            self.arrive(6)
            self.start(10)
        else:
            for k in (4, 7, 8, 9, 10):
                self.arrive(k)
            for k in range(11):
                self.finish_send(k)


def counts(g):
    return (4, 3) if g % 2 == 0 else (3, 4)


def kernel(
    owner_hbm, row_hbm, q_hbm, o_hbm, store_hbm, gain_ref, key_hbm, value_hbm,
    att_hbm, qg_hbm, kw_hbm, vw_hbm,
    owner_s, row_s, done_part, done_weights,
    every, gains, w_key, w_value, table, table_s, qo, turned, normed, held_k, held_v,
    e_buf, pg_buf, stats, moments, own_part, sent_part, came_part, f0, f1, f2, f3,
    dense, ring_up, ring_down, rows, parts, first_up, first_down, sum_up, sum_down,
    local, out_sems, store_sems, gain_sems, tab_sems, qo_sems, every_s, every_r, turn_sems, normed_s, normed_r,
    ring_sems, stat_sems, moment_sems, back_sems, part_sems, row_sems, sum_sems,
):
    z, y, m = place()
    full = (f0, f1, f2, f3)
    up, down = (wrap(z + 1, NZ), y, m), (wrap(z - 1, NZ), y, m)

    def at_y(k):
        return wrap(y + k, NY)

    def from_y(k):
        return wrap(y - k, NY)

    def peer(k):
        return (z, at_y(k), m)

    pieces = [MpGather(every, 2 * from_y(k), 2, every_s, every_r, k) for k in range(NY)]
    second_moves = MpGather(normed, 0, 128, normed_s, normed_r, 0)

    met = greet(
        [peer(k) for k in (1, 2, 3)] + [up, down] + [(z, y, wrap(m + k, NM)) for k in range(1, NM)]
    )

    def at_home():
        quarter = pl.ds(pl.multiple_of(TOK * y, TOK), TOK)
        copies = [
            pltpu.make_async_copy(store_hbm.at[:, quarter], every.at[m, pl.ds(2 * y, 2)], local.at[0]),
            pltpu.make_async_copy(key_hbm, w_key, local.at[1]),
            pltpu.make_async_copy(value_hbm, w_value, local.at[2]),
            pltpu.make_async_copy(owner_hbm, owner_s, local.at[9]),
            pltpu.make_async_copy(row_hbm, row_s, local.at[10]),
        ]
        for h in range(2):
            for i, ref in enumerate((q_hbm, o_hbm)):
                copies.append(
                    pltpu.make_async_copy(ref.at[:, pl.ds(HEAD * h, HEAD)], qo.at[h, y, i], local.at[3 + 2 * h + i])
                )
        return copies

    home = at_home()
    for i in (0, 3, 4, 1, 2, 5, 6, 7, 8):
        home[i].start()

    def store_copy(k, source, target):
        quarter = pl.ds(pl.multiple_of(TOK * target[1], TOK), TOK)
        return remote(
            store_hbm.at[:, quarter], every.at[m, pl.ds(2 * source, 2)], store_sems.at[0, k - 1], store_sems.at[1, k - 1], target
        )

    def gain_copy(k, source, target):
        return remote(gains.at[source], gains.at[source], gain_sems.at[0, k - 1], gain_sems.at[1, k - 1], (z, y, target))

    def tab_copy(k, source):
        return remote(table.at[source], table.at[source], tab_sems.at[0, k - 1], tab_sems.at[1, k - 1], peer(k))

    def qo_copy(h, i, k, source):
        ref = (q_hbm, o_hbm)[i]
        return remote(
            ref.at[:, pl.ds(HEAD * h, HEAD)], qo.at[h, source, i], qo_sems.at[0, h, i, k - 1], qo_sems.at[1, h, i, k - 1], peer(k)
        )

    met()
    for k in ORDER:
        store_copy(k, y, peer(k)).start()
    home[0].wait()
    pieces[0].step(0)

    home[3].wait()
    home[4].wait()

    lane = lax.broadcasted_iota(I32, (8, 128), 1)
    line = lax.broadcasted_iota(I32, (8, 128), 0)
    ids = jnp.zeros((8, 128), I32)
    first = jnp.full((8, 128), NONE, I32)
    last = jnp.full((8, 128), -1, I32)
    for r in range(REFS):
        name = owner_s[r % 2, r // 2] * 2 + row_s[r % 2, r // 2]
        ids = jnp.where(lane == r, name, ids)
        first = jnp.where(lane == name, jnp.minimum(first, r), first)
        last = jnp.where(lane == name, r, last)
    second = jnp.where(last > first, last, NONE)
    table[y] = jnp.where(line == 0, ids, jnp.where(line == 1, first, second))
    gains[m] = jnp.broadcast_to(gain_ref[...].reshape(1, 512), (16, 512))
    for g in range(4):
        full[g][:, NONE] = jnp.zeros((NY, TOK, HEAD), F32)
    moments[y] = jnp.zeros((2, NY, 8, 128), F32)

    for k in range(1, NM):
        gain_copy(k, m, wrap(m + k, NM)).start()
    for k in ORDER:
        tab_copy(k, y).start()

    def encode(k):
        first = 2 * from_y(k)
        total = jnp.zeros((64, 1), F32)
        for j in range(NM):
            part = every[j, pl.ds(first, 2)].reshape(64, 512).astype(F32)
            total += jnp.sum(part * part, axis=-1, keepdims=True)
        scale = lax.rsqrt(total * (1.0 / 4096.0) + EPS)
        keys, values = jnp.zeros((64, 256), F32), jnp.zeros((64, 256), F32)
        for j in range(NM):
            gain = gains[j][0:1].astype(F32)
            rows_of = (every[j, pl.ds(first, 2)].reshape(64, 512).astype(F32) * scale * gain).astype(BF16)
            every[j, pl.ds(first, 2)] = rows_of.reshape(2, TOK, 512)
            depth = slice(512 * j, 512 * (j + 1))
            keys += jnp.dot(rows_of, w_key[depth], preferred_element_type=F32)
            values += jnp.dot(rows_of, w_value[depth], preferred_element_type=F32)
        for h in range(2):
            for held, encoded in ((held_k, keys), (held_v, values)):
                part = encoded[:, HEAD * h : HEAD * (h + 1)].astype(BF16)
                held[h, pl.ds(8 * z + first, 2)] = part.reshape(2, TOK, HEAD)

    def ring_copy(k, i, direction, h, block):
        piece = (held_k, held_v)[i].at[:, pl.ds(8 * block + 2 * from_y(k), 2)]
        sems = [ring_sems.at[end, 4 * i + k, direction, h] for end in (0, 1)]
        return remote(piece, piece, sems[0], sems[1], (up, down)[direction])

    def ring_sent(k, i, direction, h):
        return ring_copy(k, i, direction, h, wrap(z - h, NZ) if direction == 0 else wrap(z + h, NZ))

    def ring_came(k, i, direction, h):
        return ring_copy(k, i, direction, h, wrap(z - 1 - h, NZ) if direction == 0 else wrap(z + 1 + h, NZ))

    def launch(k, i):
        for direction in (0, 1):
            ring_sent(k, i, direction, 0).start()

    def advance(k, i, h):
        for direction in (0, 1):
            if h < counts(k)[direction]:
                ring_came(k, i, direction, h).wait_recv()
                if h + 1 < counts(k)[direction]:
                    ring_sent(k, i, direction, h + 1).start()

    def turn_copy(k, source):
        lanes = pl.ds(pl.multiple_of(256 * source, 256), 256)
        return remote(
            turned.at[at_y(k)], normed.at[m, :, lanes], turn_sems.at[0, k - 1], turn_sems.at[1, k - 1], peer(k)
        )

    def turn():
        flat = every[m].reshape(256, 512).astype(F32).T.astype(BF16)
        for i in range(NY):
            turned[i] = flat[128 * i : 128 * (i + 1)]
        for k in ORDER:
            turn_copy(k, y).start()
        copy = pltpu.make_async_copy(turned.at[y], normed.at[m, :, pl.ds(pl.multiple_of(256 * y, 256), 256)], local.at[8])
        copy.start()
        copy.wait()

    context_span = lax.div(lax.broadcasted_iota(I32, (128, 128), 0), 64)
    query_span = lax.div(lax.broadcasted_iota(I32, (128, 128), 1), 64)
    same = context_span == query_span

    def context(held, h, b, p):
        return jnp.concatenate([held[h, table_s[b, 0, 4 * p + i]] for i in range(4)], axis=0)

    def score(h, k):
        b = at_y(k)
        for p in range(4):
            queries = qo[h, b, 0, 128 * p : 128 * (p + 1)]
            scores = lax.dot_general(context(held_k, h, b, p), queries, DOWN, preferred_element_type=F32) * ROOT
            scores = jnp.where(same, scores, FLOOR)
            top = jnp.max(scores, axis=0, keepdims=True)
            weights = jnp.exp(scores - top)
            e_buf[h, k, p] = weights
            stats[y, h, b, p : p + 1] = top
            stats[y, h, b, 4 + p : 5 + p] = jnp.sum(weights, axis=0, keepdims=True)

    def stat_copy(k, source):
        piece = stats.at[source]
        return remote(piece, piece, stat_sems.at[0, k - 1], stat_sems.at[1, k - 1], peer(k))

    def moment_copy(k, source):
        piece = moments.at[source]
        return remote(piece, piece, moment_sems.at[0, k - 1], moment_sems.at[1, k - 1], peer(k))

    def part_copy(h, i, k):
        return remote(
            sent_part.at[h, i, k - 1], came_part.at[h, i, k - 1], part_sems.at[0, h, i, k - 1], part_sems.at[1, h, i, k - 1], peer(k)
        )

    def keep(h, i, k, lines, value):
        if k == 0:
            own_part[h, i, lines] = value
        else:
            sent_part[h, i, k - 1, lines] = value.astype(BF16)

    def attend(h, k):
        b = at_y(k)
        tops = [stats[s, h, b, 0:4] for s in range(NY)]
        top = jnp.maximum(jnp.maximum(tops[0], tops[1]), jnp.maximum(tops[2], tops[3]))
        whole = jnp.zeros((4, 128), F32)
        for s in range(NY):
            whole += jnp.exp(tops[s] - top) * stats[s, h, b, 4:8]
        factor = jnp.exp(stats[y, h, b, 0:4] - top) / whole
        for p in range(4):
            lines = slice(128 * p, 128 * (p + 1))
            grads = qo[h, b, 1, lines]
            values = context(held_v, h, b, p)
            probs = e_buf[h, k, p] * factor[p : p + 1]
            low = probs.astype(BF16)
            prob_grad = lax.dot_general(values, grads, DOWN, preferred_element_type=F32)
            e_buf[h, k, p] = probs
            pg_buf[h, k, p] = prob_grad
            moments[y, h, b, p : p + 1] = jnp.sum(probs * prob_grad, axis=0, keepdims=True)
            keep(h, 0, k, lines, lax.dot_general(low, values, ACROSS, preferred_element_type=F32))
            value_grad = jnp.dot(low, grads, preferred_element_type=F32)
            full[h][b, 4 * p : 4 * p + 4] = value_grad.reshape(4, TOK, HEAD)

    def grads_of(h, k):
        b = at_y(k)
        delta = (moments[0, h, b, 0:4] + moments[1, h, b, 0:4]) + (moments[2, h, b, 0:4] + moments[3, h, b, 0:4])
        for p in range(4):
            lines = slice(128 * p, 128 * (p + 1))
            score_grad = (e_buf[h, k, p] * (pg_buf[h, k, p] - delta[p : p + 1])).astype(BF16)
            keys = context(held_k, h, b, p)
            keep(h, 1, k, lines, lax.dot_general(score_grad, keys, ACROSS, preferred_element_type=F32) * ROOT)
            key_grad = jnp.dot(score_grad, qo[h, b, 0, lines], preferred_element_type=F32) * ROOT
            full[2 + h][b, 4 * p : 4 * p + 4] = key_grad.reshape(4, TOK, HEAD)

    def send_parts(h, i):
        for k in ORDER:
            part_copy(h, i, k).start()

    def outputs(h, i):
        for k in ORDER:
            part_copy(h, i, k).wait_recv()
        whole = own_part[h, i]
        for k in ORDER:
            whole += came_part[h, i, k - 1].astype(F32)
        done_part[h, i] = whole.astype(BF16)
        part_out(h, i).start()

    def part_out(h, i):
        ref = (att_hbm, qg_hbm)[i]
        return pltpu.make_async_copy(done_part.at[h, i], ref.at[:, pl.ds(HEAD * h, HEAD)], out_sems.at[2 * h + i])

    def block(dest):
        return pl.ds(8 * wrap(dest, NZ), 8)

    def back_copy(g, direction, h):
        buffers, target = ((ring_up, up), (ring_down, down))[direction]
        count = counts(g)[direction]
        if h == 0:
            src = dense.at[g, block(z + count if direction == 0 else z - count)]
        else:
            src = buffers.at[g, h - 1]
        return remote(src, buffers.at[g, h], back_sems.at[0, g, direction, h], back_sems.at[1, g, direction, h], target)

    def add_up(g):
        def body(s, carry):
            whole = full[g][0, table_s[0, 1, s]] + full[g][0, table_s[0, 2, s]]
            for b in range(1, NY):
                whole += full[g][b, table_s[b, 1, s]] + full[g][b, table_s[b, 2, s]]
            dense[g, s] = whole.astype(BF16)
            return carry

        lax.fori_loop(0, 64, body, 0, unroll=4)
        for direction in (0, 1):
            back_copy(g, direction, 0).start()

    def pass_back(g, h):
        for direction in (0, 1):
            count = counts(g)[direction]
            if h < count - 1:
                buffers = (ring_up, ring_down)[direction]
                back_copy(g, direction, h).wait_recv()
                dest = z + (count - 1 - h) if direction == 0 else z - (count - 1 - h)
                buffers[g, h] = (buffers[g, h].astype(F32) + dense[g, block(dest)].astype(F32)).astype(BF16)
                back_copy(g, direction, h + 1).start()

    def row_copy(g, k, source):
        piece = rows.at[source, g]
        return remote(piece, piece, row_sems.at[0, g, k - 1], row_sems.at[1, g, k - 1], peer(k))

    def settle(g):
        n_up, n_down = counts(g)
        back_copy(g, 0, n_up - 1).wait_recv()
        back_copy(g, 1, n_down - 1).wait_recv()
        whole = dense[g, block(z)].astype(F32) + ring_up[g, n_up - 1].astype(F32) + ring_down[g, n_down - 1].astype(F32)
        rows[y, g] = whole.astype(BF16).reshape(256, HEAD)
        for k in ORDER:
            row_copy(g, k, y).start()

    def sum_copy(g, direction, n):
        buffers, firsts, target = ((sum_up, first_up, up), (sum_down, first_down, down))[direction]
        src = firsts.at[g] if n == 0 else buffers.at[g, n - 1]
        return remote(src, buffers.at[g, n], sum_sems.at[0, g, direction, n], sum_sems.at[1, g, direction, n], target)

    def weigh(g):
        for k in ORDER:
            row_copy(g, k, from_y(k)).wait_recv()
        row_grad = jnp.concatenate([rows[s, g] for s in range(NY)], axis=0)

        def partial_of(dest):
            return jnp.dot(normed[wrap(dest, NZ)], row_grad, preferred_element_type=F32)

        n_up, n_down = counts(g)
        for direction in (g % 2, 1 - g % 2):
            if direction == 0:
                first_up[g] = partial_of(z + n_up).astype(BF16)
            else:
                first_down[g] = partial_of(z - n_down).astype(BF16)
            sum_copy(g, direction, 0).start()
        for offset in (3, -3, 2, -2, 1, -1, 0):
            if offset not in (n_up, -n_down):
                parts[g, wrap(z + offset, NZ)] = partial_of(z + offset)

    def pass_sum(g, n):
        for direction in (g % 2, 1 - g % 2):
            count = counts(g)[direction]
            if n < count - 1:
                buffers = (sum_up, sum_down)[direction]
                sum_copy(g, direction, n).wait_recv()
                dest = z + (count - 1 - n) if direction == 0 else z - (count - 1 - n)
                buffers[g, n] = (buffers[g, n].astype(F32) + parts[g, wrap(dest, NZ)]).astype(BF16)
                sum_copy(g, direction, n + 1).start()

    def weights_out(g):
        n_up, n_down = counts(g)
        sum_copy(g, 0, n_up - 1).wait_recv()
        sum_copy(g, 1, n_down - 1).wait_recv()
        whole = parts[g, z] + sum_up[g, n_up - 1].astype(F32) + sum_down[g, n_down - 1].astype(F32)
        done_weights[g] = whole
        weight_out(g).start()

    def weight_out(g):
        ref = (vw_hbm, kw_hbm)[g // 2]
        return pltpu.make_async_copy(done_weights.at[g], ref.at[:, pl.ds(HEAD * (g % 2), HEAD)], out_sems.at[4 + g])

    def arrive(k):
        store_copy(k, from_y(k), (z, y, m)).wait_recv()
        pieces[k].step(0)

    def send_queries():
        for h in range(2):
            for k in ORDER:
                for i in range(2):
                    qo_copy(h, i, k, y).start()

    def weights_here():
        for k in range(1, NM):
            gain_copy(k, wrap(m - k, NM), m).wait_recv()
        home[1].wait()
        home[2].wait()

    def finish_piece(k):
        pieces[k].step(4)
        encode(k)
        launch(k, 0)
        launch(k, 1)

    go = functools.partial
    plan = [(4.3, go(arrive, 1)), (4.5, go(arrive, 3)), (6.3, go(arrive, 2)), (6.4, send_queries), (7.0, weights_here), (17.2, turn)]
    for k, steps in ((0, (3.7, 4.4, 6.8, 8.2)), (1, (8.0, 8.7, 11.0, 12.5)), (3, (8.6, 9.3, 11.7, 13.3)), (2, (10.5, 11.2, 13.5, 15.0))):
        for number in range(3):
            plan.append((steps[number], go(pieces[k].step, number + 1)))
        plan.append((steps[3], go(finish_piece, k)))
        for h in range(4):
            due = steps[3] + 2.0 + 3.4 * (h + 1)
            plan.append((due, go(advance, k, 0, h)))
            plan.append((due + 2.0, go(advance, k, 1, h)))

    def scalars_here():
        for k in ORDER:
            tab_copy(k, from_y(k)).wait_recv()
        to_scalars = pltpu.make_async_copy(table, table_s, local.at[7])
        to_scalars.start()
        for copy in home[5:]:
            copy.wait()
        to_scalars.wait()

    def queries_here(h):
        for i in range(2):
            for k in ORDER:
                qo_copy(h, i, k, from_y(k)).wait_recv()

    def send_stats():
        for k in ORDER:
            stat_copy(k, y).start()

    def stats_here():
        for k in ORDER:
            stat_copy(k, from_y(k)).wait_recv()

    def send_moments():
        for k in ORDER:
            moment_copy(k, y).start()

    def moments_here():
        for k in ORDER:
            moment_copy(k, from_y(k)).wait_recv()

    def turned_here():
        for k in ORDER:
            turn_copy(k, from_y(k)).wait_recv()

    due = 15.0 + 2.0 + 3.4 * 4 + 0.1
    plan += [(due, scalars_here), (due, go(queries_here, 0)), (due, go(queries_here, 1))]
    plan += [(due, go(score, h, k)) for h in range(2) for k in range(NY)] + [(due, send_stats)]
    steps = [action for _, action in sorted(plan, key=lambda entry: entry[0])]
    steps += [stats_here] + [go(attend, 0, k) for k in range(NY)] + [go(add_up, 0)]
    steps += [go(attend, 1, k) for k in range(NY)] + [send_moments, go(add_up, 1), go(send_parts, 0, 0), go(send_parts, 1, 0)]
    steps += [turned_here, go(second_moves.step, 0), go(pass_back, 0, 0), go(pass_back, 1, 0), moments_here]
    for h in range(2):
        steps += [go(grads_of, h, k) for k in range(NY)] + [go(add_up, 2 + h)]
    steps += [go(send_parts, 0, 1), go(pass_back, 0, 1), go(pass_back, 1, 1), go(second_moves.step, 1)]
    steps += [go(pass_back, 2, 0), go(pass_back, 3, 0), go(pass_back, 0, 2), go(pass_back, 1, 2), go(second_moves.step, 2)]
    steps += [go(pass_back, 2, 1), go(pass_back, 3, 1), go(settle, 0), go(settle, 1), go(second_moves.step, 3)]
    steps += [go(pass_back, 2, 2), go(pass_back, 3, 2), go(second_moves.step, 4), go(outputs, 0, 0), go(settle, 2), go(settle, 3)]
    steps += [go(send_parts, 1, 1), go(outputs, 1, 0), go(weigh, 0), go(weigh, 1), go(pass_sum, 0, 0), go(pass_sum, 1, 0)]
    steps += [go(weigh, 2), go(pass_sum, 0, 1), go(pass_sum, 1, 1), go(weigh, 3), go(pass_sum, 0, 2), go(pass_sum, 1, 2)]
    steps += [go(pass_sum, 2, 0), go(pass_sum, 3, 0), go(weights_out, 0), go(weights_out, 1), go(pass_sum, 2, 1), go(pass_sum, 3, 1)]
    steps += [go(outputs, 0, 1), go(pass_sum, 2, 2), go(pass_sum, 3, 2), go(weights_out, 2), go(weights_out, 3), go(outputs, 1, 1)]
    for action in steps:
        action()

    for h in range(2):
        for i in range(2):
            part_out(h, i).wait()
    for g in range(4):
        weight_out(g).wait()
    for k in ORDER:
        store_copy(k, y, peer(k)).wait_send()
        tab_copy(k, y).wait_send()
        turn_copy(k, y).wait_send()
        stat_copy(k, y).wait_send()
        moment_copy(k, y).wait_send()
        for h in range(2):
            for i in range(2):
                qo_copy(h, i, k, y).wait_send()
                part_copy(h, i, k).wait_send()
        for g in range(4):
            row_copy(g, k, y).wait_send()
    for k in range(1, NM):
        gain_copy(k, m, wrap(m + k, NM)).wait_send()
    for direction in (0, 1):
        for g in range(4):
            for n in range(counts(g)[direction]):
                ring_sent(g, 0, direction, n).wait_send()
                ring_sent(g, 1, direction, n).wait_send()
                back_copy(g, direction, n).wait_send()
                sum_copy(g, direction, n).wait_send()


def hand_over(*refs):
    for source, target in zip(refs[:4], refs[4:]):
        target[...] = source[...]


def dma(*shape):
    return pltpu.SemaphoreType.DMA(shape)


def shards(queries, out_grad, owner, store_row, store, norm_gain, w_key, w_value):
    in_vmem, anywhere = (pl.BlockSpec(memory_space=space) for space in (VMEM, pl.ANY))
    tile = (TOK, HEAD)
    results = pl.pallas_call(
        kernel,
        out_shape=(
            jax.ShapeDtypeStruct((512, 256), BF16),
            jax.ShapeDtypeStruct((512, 256), BF16),
            jax.ShapeDtypeStruct((128, 256), F32),
            jax.ShapeDtypeStruct((128, 256), F32),
        ),
        in_specs=[anywhere, anywhere, anywhere, anywhere, anywhere, in_vmem, anywhere, anywhere],
        out_specs=(anywhere,) * 4,
        scratch_shapes=[
            SMEM((2, 8), I32),
            SMEM((2, 8), I32),
            VMEM((2, 2, 512, HEAD), BF16),
            VMEM((4, 128, HEAD), F32),
            VMEM((NM, 8, TOK, 512), BF16),
            VMEM((NM, 16, 512), BF16),
            VMEM((4096, 256), BF16),
            VMEM((4096, 256), BF16),
            VMEM((NY, 8, 128), I32),
            SMEM((NY, 8, 128), I32),
            VMEM((2, NY, 2, 512, HEAD), BF16),
            VMEM((NY, 128, 256), BF16),
            VMEM((NM, 128, 1024), BF16),
            VMEM((2, 64) + tile, BF16),
            VMEM((2, 64) + tile, BF16),
            VMEM((2, NY, 4, 128, 128), F32),
            VMEM((2, NY, 4, 128, 128), F32),
            VMEM((NY, 2, NY, 8, 128), F32),
            VMEM((NY, 2, NY, 8, 128), F32),
            VMEM((2, 2, 512, HEAD), F32),
            VMEM((2, 2, 3, 512, HEAD), BF16),
            VMEM((2, 2, 3, 512, HEAD), BF16),
        ]
        + [VMEM((NY, REFS + 1) + tile, F32)] * 4
        + [
            VMEM((4, 64) + tile, BF16),
            VMEM((4, 4, 8) + tile, BF16),
            VMEM((4, 4, 8) + tile, BF16),
            VMEM((NY, 4, 256, HEAD), BF16),
            VMEM((4, NZ, 128, HEAD), F32),
            VMEM((4, 128, HEAD), BF16),
            VMEM((4, 128, HEAD), BF16),
            VMEM((4, 4, 128, HEAD), BF16),
            VMEM((4, 4, 128, HEAD), BF16),
            dma(11), dma(8), dma(2, 3), dma(2, 7), dma(2, 3), dma(2, 2, 2, 3), dma(4, 11), dma(4, 11), dma(2, 3), dma(1, 11), dma(1, 11),
            dma(2, 8, 2, 4), dma(2, 3), dma(2, 3), dma(2, 4, 2, 4), dma(2, 2, 2, 3), dma(2, 4, 3), dma(2, 4, 2, 4),
        ],
        compiler_params=pltpu.CompilerParams(
            collective_id=0, has_side_effects=True, vmem_limit_bytes=60 * 1024 * 1024
        ),
        name="spans",
    )(owner.T, store_row.T, queries, out_grad, store, norm_gain, w_key, w_value)
    return pl.pallas_call(
        hand_over,
        out_shape=tuple(jax.ShapeDtypeStruct(each.shape, each.dtype) for each in results),
        in_specs=[in_vmem] * 4,
        out_specs=(in_vmem,) * 4,
        name="hand_over",
    )(*results)


def solution(mesh):
    in_specs = (
        P("dp", "mp"),
        P("dp", "mp"),
        P("dp", None),
        P("dp", None),
        P("dp", None, "mp"),
        P("mp"),
        P(None, "mp"),
        P(None, "mp"),
    )
    out_specs = (P("dp", "mp"), P("dp", "mp"), P("dp", "mp"), P("dp", "mp"))
    return jax.shard_map(shards, mesh=mesh, in_specs=in_specs, out_specs=out_specs, check_vma=False)
```

```python
import functools
import math

import jax
import jax.numpy as jnp
from jax import lax
from jax.experimental import pallas as pl
from jax.experimental.pallas import tpu as pltpu
from jax.sharding import PartitionSpec as P

MESH = pl.DeviceIdType.MESH
VMEM, SMEM = pltpu.VMEM, pltpu.SMEM
F32, BF16, I32 = jnp.float32, jnp.bfloat16, jnp.int32

HEAD = 128
ROOT = 1.0 / math.sqrt(HEAD)
EPS = 1e-06
NZ, NY, NM = 8, 4, 8
TOK = 32
REFS = 16
NONE = REFS
FLOOR = -3.0e38
DOWN = (((1,), (1,)), ((), ()))
ACROSS = (((0,), (0,)), ((), ()))
ORDER = (1, 3, 2)


def wrap(value, size):
    return lax.rem(value + size, size)


def place():
    d, m = lax.axis_index("dp"), lax.axis_index("mp")
    return lax.div(d, NY), lax.rem(d, NY), m


def remote(src, dst, send, recv, target):
    z, y, m = target
    return pltpu.make_async_remote_copy(
        src_ref=src, dst_ref=dst, send_sem=send, recv_sem=recv, device_id=(z * NY + y, m), device_id_type=MESH
    )


def greet(peers):
    barrier = pltpu.get_barrier_semaphore()
    for z, y, m in peers:
        pl.semaphore_signal(barrier, inc=1, device_id=(z * NY + y, m), device_id_type=MESH)
    return lambda: pl.semaphore_wait(barrier, len(peers))


class MpGather:
    def __init__(self, ref, base, size, send, recv, number):
        self.ref, self.send, self.recv, self.number = ref, send, recv, number
        self.z, self.y, self.m = place()
        self.right, self.left, self.opposite = wrap(self.m + 2, NM), wrap(self.m - 2, NM), wrap(self.m + 4, NM)
        self.twin = self.m + 1 - 2 * lax.rem(self.m, 2)
        self.low, self.high, self.whole = (base, size // 2), (base + size // 2, size // 2), (base, size)

    def copy(self, block, part, target, k):
        piece = self.ref.at[block, pl.ds(*part)]
        return remote(piece, piece, self.send.at[self.number, k], self.recv.at[self.number, k], (self.z, self.y, target))

    def sent(self):
        m, left, right, opposite = self.m, self.left, self.right, self.opposite
        return [
            (m, self.low, right), (m, self.high, right), (m, self.high, left), (m, self.low, left), (m, self.whole, self.twin),
            (left, self.low, right), (right, self.high, left),
            (left, self.whole, self.twin), (right, self.whole, self.twin),
            (opposite, self.low, self.twin), (opposite, self.high, self.twin),
        ]

    def came(self):
        left, right, opposite, twin = self.left, self.right, self.opposite, self.twin
        tl, tr, to = wrap(twin - 2, NM), wrap(twin + 2, NM), wrap(twin + 4, NM)
        return [
            (left, self.low), (left, self.high), (right, self.high), (right, self.low), (twin, self.whole),
            (opposite, self.low), (opposite, self.high),
            (tl, self.whole), (tr, self.whole), (to, self.low), (to, self.high),
        ]

    def start(self, k):
        block, part, target = self.sent()[k]
        self.copy(block, part, target, k).start()

    def arrive(self, k):
        block, part = self.came()[k]
        self.copy(block, part, self.twin, k).wait_recv()

    def finish_send(self, k):
        block, part, target = self.sent()[k]
        self.copy(block, part, target, k).wait_send()

    def step(self, number):
        if number == 0:
            for k in (0, 2, 1, 3, 4):
                self.start(k)
        elif number == 1:
            self.arrive(0)
            self.start(5)
            self.arrive(2)
            self.start(6)
        elif number == 2:
            self.arrive(1)
            self.start(7)
            self.arrive(3)
            self.start(8)
        elif number == 3:
            self.arrive(5)
            self.start(9)
            self.arrive(6)
            self.start(10)
        else:
            for k in (4, 7, 8, 9, 10):
                self.arrive(k)

    def finish(self):
        for k in range(11):
            self.finish_send(k)


def counts(g):
    return (4, 3) if g % 2 == 0 else (3, 4)


def kernel(
    owner_hbm, row_hbm, q_hbm, o_hbm, store_hbm, gain_ref, key_hbm, value_hbm,
    att_hbm, qg_hbm, kw_hbm, vw_hbm,
    owner_s, row_s, done_part, done_weights,
    every, kept, gains, w_key, w_value, table, table_s, qo, turned, normed, held_k, held_v,
    e_buf, pg_buf, stats, moments, own_part, sent_part, came_part, f0, f1, f2, f3,
    dense, ring_up, ring_down, rows, parts, first_up, first_down, sum_up, sum_down,
    local, out_sems, store_sems, gain_sems, tab_sems, qo_sems, every_s, every_r, turn_sems, normed_s, normed_r,
    ring_sems, stat_sems, moment_sems, back_sems, part_sems, row_sems, sum_sems,
):
    z, y, m = place()
    full = (f0, f1, f2, f3)
    up, down = (wrap(z + 1, NZ), y, m), (wrap(z - 1, NZ), y, m)

    def at_y(k):
        return wrap(y + k, NY)

    def from_y(k):
        return wrap(y - k, NY)

    def peer(k):
        return (z, at_y(k), m)

    pieces = [MpGather(every, 2 * from_y(k), 2, every_s, every_r, k) for k in range(NY)]
    second_moves = MpGather(normed, 0, 128, normed_s, normed_r, 0)

    met = greet(
        [peer(k) for k in (1, 2, 3)] + [up, down] + [(z, y, wrap(m + k, NM)) for k in range(1, NM)]
    )

    def at_home():
        quarter = pl.ds(pl.multiple_of(TOK * y, TOK), TOK)
        copies = [
            pltpu.make_async_copy(store_hbm.at[:, quarter], every.at[m, pl.ds(2 * y, 2)], local.at[0]),
            pltpu.make_async_copy(key_hbm, w_key, local.at[1]),
            pltpu.make_async_copy(value_hbm, w_value, local.at[2]),
            pltpu.make_async_copy(owner_hbm, owner_s, local.at[9]),
            pltpu.make_async_copy(row_hbm, row_s, local.at[10]),
        ]
        for h in range(2):
            for i, ref in enumerate((q_hbm, o_hbm)):
                copies.append(
                    pltpu.make_async_copy(ref.at[:, pl.ds(HEAD * h, HEAD)], qo.at[h, y, i], local.at[3 + 2 * h + i])
                )
        return copies

    home = at_home()
    for i in (0, 3, 4, 1, 2, 5, 6, 7, 8):
        home[i].start()

    def store_copy(k, source, target):
        quarter = pl.ds(pl.multiple_of(TOK * target[1], TOK), TOK)
        return remote(
            store_hbm.at[:, quarter], every.at[m, pl.ds(2 * source, 2)], store_sems.at[0, k - 1], store_sems.at[1, k - 1], target
        )

    def gain_copy(k, source, target):
        return remote(gains.at[source], gains.at[source], gain_sems.at[0, k - 1], gain_sems.at[1, k - 1], (z, y, target))

    def tab_copy(k, source):
        return remote(table.at[source], table.at[source], tab_sems.at[0, k - 1], tab_sems.at[1, k - 1], peer(k))

    def qo_copy(h, i, k, source):
        ref = (q_hbm, o_hbm)[i]
        return remote(
            ref.at[:, pl.ds(HEAD * h, HEAD)], qo.at[h, source, i], qo_sems.at[0, h, i, k - 1], qo_sems.at[1, h, i, k - 1], peer(k)
        )

    met()
    for k in ORDER:
        store_copy(k, y, peer(k)).start()
    home[0].wait()
    pieces[0].step(0)

    home[3].wait()
    home[4].wait()

    lane = lax.broadcasted_iota(I32, (8, 128), 1)
    line = lax.broadcasted_iota(I32, (8, 128), 0)
    ids = jnp.zeros((8, 128), I32)
    first = jnp.full((8, 128), NONE, I32)
    last = jnp.full((8, 128), -1, I32)
    for r in range(REFS):
        name = owner_s[r % 2, r // 2] * 2 + row_s[r % 2, r // 2]
        ids = jnp.where(lane == r, name, ids)
        first = jnp.where(lane == name, jnp.minimum(first, r), first)
        last = jnp.where(lane == name, r, last)
    second = jnp.where(last > first, last, NONE)
    table[y] = jnp.where(line == 0, ids, jnp.where(line == 1, first, second))
    gains[m] = jnp.broadcast_to(gain_ref[...].reshape(1, 512), (16, 512))
    for g in range(4):
        full[g][:, NONE] = jnp.zeros((NY, TOK, HEAD), F32)
    moments[y] = jnp.zeros((2, NY, 8, 128), F32)

    for k in range(1, NM):
        gain_copy(k, m, wrap(m + k, NM)).start()
    for k in ORDER:
        tab_copy(k, y).start()

    def encode(k):
        first = 2 * from_y(k)
        total = jnp.zeros((64, 1), F32)
        for j in range(NM):
            part = every[j, pl.ds(first, 2)].reshape(64, 512).astype(F32)
            total += jnp.sum(part * part, axis=-1, keepdims=True)
        scale = lax.rsqrt(total * (1.0 / 4096.0) + EPS)
        keys, values = jnp.zeros((64, 256), F32), jnp.zeros((64, 256), F32)
        for j in range(NM):
            gain = gains[j][0:1].astype(F32)
            rows_of = (every[j, pl.ds(first, 2)].reshape(64, 512).astype(F32) * scale * gain).astype(BF16)
            kept[j, pl.ds(first, 2)] = rows_of.reshape(2, TOK, 512)
            depth = slice(512 * j, 512 * (j + 1))
            keys += jnp.dot(rows_of, w_key[depth], preferred_element_type=F32)
            values += jnp.dot(rows_of, w_value[depth], preferred_element_type=F32)
        for h in range(2):
            for held, encoded in ((held_k, keys), (held_v, values)):
                part = encoded[:, HEAD * h : HEAD * (h + 1)].astype(BF16)
                held[h, pl.ds(8 * z + first, 2)] = part.reshape(2, TOK, HEAD)

    def ring_copy(k, i, direction, h, block):
        piece = (held_k, held_v)[i].at[:, pl.ds(8 * block + 2 * from_y(k), 2)]
        sems = [ring_sems.at[end, 4 * i + k, direction, h] for end in (0, 1)]
        return remote(piece, piece, sems[0], sems[1], (up, down)[direction])

    def ring_sent(k, i, direction, h):
        return ring_copy(k, i, direction, h, wrap(z - h, NZ) if direction == 0 else wrap(z + h, NZ))

    def ring_came(k, i, direction, h):
        return ring_copy(k, i, direction, h, wrap(z - 1 - h, NZ) if direction == 0 else wrap(z + 1 + h, NZ))

    def launch(k, i):
        for direction in (0, 1):
            ring_sent(k, i, direction, 0).start()

    def advance(k, i, h):
        for direction in (0, 1):
            if h < counts(k)[direction]:
                ring_came(k, i, direction, h).wait_recv()
                if h + 1 < counts(k)[direction]:
                    ring_sent(k, i, direction, h + 1).start()

    def turn_copy(k, source):
        lanes = pl.ds(pl.multiple_of(256 * source, 256), 256)
        return remote(
            turned.at[at_y(k)], normed.at[m, :, lanes], turn_sems.at[0, k - 1], turn_sems.at[1, k - 1], peer(k)
        )

    def turn():
        flat = kept[m].reshape(256, 512).astype(F32).T.astype(BF16)
        for i in range(NY):
            turned[i] = flat[128 * i : 128 * (i + 1)]
        for k in ORDER:
            turn_copy(k, y).start()
        copy = pltpu.make_async_copy(turned.at[y], normed.at[m, :, pl.ds(pl.multiple_of(256 * y, 256), 256)], local.at[8])
        copy.start()
        copy.wait()

    context_span = lax.div(lax.broadcasted_iota(I32, (128, 128), 0), 64)
    query_span = lax.div(lax.broadcasted_iota(I32, (128, 128), 1), 64)
    same = context_span == query_span

    def context(held, h, b, p):
        return jnp.concatenate([held[h, table_s[b, 0, 4 * p + i]] for i in range(4)], axis=0)

    def score(h, k):
        b = at_y(k)
        for p in range(4):
            queries = qo[h, b, 0, 128 * p : 128 * (p + 1)]
            scores = lax.dot_general(context(held_k, h, b, p), queries, DOWN, preferred_element_type=F32) * ROOT
            scores = jnp.where(same, scores, FLOOR)
            top = jnp.max(scores, axis=0, keepdims=True)
            weights = jnp.exp(scores - top)
            e_buf[h, k, p] = weights
            stats[y, h, b, p : p + 1] = top
            stats[y, h, b, 4 + p : 5 + p] = jnp.sum(weights, axis=0, keepdims=True)

    def stat_copy(k, source):
        piece = stats.at[source]
        return remote(piece, piece, stat_sems.at[0, k - 1], stat_sems.at[1, k - 1], peer(k))

    def moment_copy(k, source):
        piece = moments.at[source]
        return remote(piece, piece, moment_sems.at[0, k - 1], moment_sems.at[1, k - 1], peer(k))

    def part_copy(h, i, k):
        return remote(
            sent_part.at[h, i, k - 1], came_part.at[h, i, k - 1], part_sems.at[0, h, i, k - 1], part_sems.at[1, h, i, k - 1], peer(k)
        )

    def keep(h, i, k, lines, value):
        if k == 0:
            own_part[h, i, lines] = value
        else:
            sent_part[h, i, k - 1, lines] = value.astype(BF16)

    def attend(h, k):
        b = at_y(k)
        tops = [stats[s, h, b, 0:4] for s in range(NY)]
        top = jnp.maximum(jnp.maximum(tops[0], tops[1]), jnp.maximum(tops[2], tops[3]))
        whole = jnp.zeros((4, 128), F32)
        for s in range(NY):
            whole += jnp.exp(tops[s] - top) * stats[s, h, b, 4:8]
        factor = jnp.exp(stats[y, h, b, 0:4] - top) / whole
        for p in range(4):
            lines = slice(128 * p, 128 * (p + 1))
            grads = qo[h, b, 1, lines]
            values = context(held_v, h, b, p)
            probs = e_buf[h, k, p] * factor[p : p + 1]
            low = probs.astype(BF16)
            prob_grad = lax.dot_general(values, grads, DOWN, preferred_element_type=F32)
            e_buf[h, k, p] = probs
            pg_buf[h, k, p] = prob_grad
            moments[y, h, b, p : p + 1] = jnp.sum(probs * prob_grad, axis=0, keepdims=True)
            keep(h, 0, k, lines, lax.dot_general(low, values, ACROSS, preferred_element_type=F32))
            value_grad = jnp.dot(low, grads, preferred_element_type=F32)
            full[h][b, 4 * p : 4 * p + 4] = value_grad.reshape(4, TOK, HEAD)

    def grads_of(h, k):
        b = at_y(k)
        delta = (moments[0, h, b, 0:4] + moments[1, h, b, 0:4]) + (moments[2, h, b, 0:4] + moments[3, h, b, 0:4])
        for p in range(4):
            lines = slice(128 * p, 128 * (p + 1))
            score_grad = (e_buf[h, k, p] * (pg_buf[h, k, p] - delta[p : p + 1])).astype(BF16)
            keys = context(held_k, h, b, p)
            keep(h, 1, k, lines, lax.dot_general(score_grad, keys, ACROSS, preferred_element_type=F32) * ROOT)
            key_grad = jnp.dot(score_grad, qo[h, b, 0, lines], preferred_element_type=F32) * ROOT
            full[2 + h][b, 4 * p : 4 * p + 4] = key_grad.reshape(4, TOK, HEAD)

    def send_parts(h, i):
        for k in ORDER:
            part_copy(h, i, k).start()

    def outputs(h, i):
        for k in ORDER:
            part_copy(h, i, k).wait_recv()
        whole = own_part[h, i]
        for k in ORDER:
            whole += came_part[h, i, k - 1].astype(F32)
        done_part[h, i] = whole.astype(BF16)
        part_out(h, i).start()

    def part_out(h, i):
        ref = (att_hbm, qg_hbm)[i]
        return pltpu.make_async_copy(done_part.at[h, i], ref.at[:, pl.ds(HEAD * h, HEAD)], out_sems.at[2 * h + i])

    def block(dest):
        return pl.ds(8 * wrap(dest, NZ), 8)

    def back_copy(g, direction, h):
        buffers, target = ((ring_up, up), (ring_down, down))[direction]
        count = counts(g)[direction]
        if h == 0:
            src = dense.at[g, block(z + count if direction == 0 else z - count)]
        else:
            src = buffers.at[g, h - 1]
        return remote(src, buffers.at[g, h], back_sems.at[0, g, direction, h], back_sems.at[1, g, direction, h], target)

    def add_up(g):
        def body(s, carry):
            whole = full[g][0, table_s[0, 1, s]] + full[g][0, table_s[0, 2, s]]
            for b in range(1, NY):
                whole += full[g][b, table_s[b, 1, s]] + full[g][b, table_s[b, 2, s]]
            dense[g, s] = whole.astype(BF16)
            return carry

        lax.fori_loop(0, 64, body, 0, unroll=4)
        for direction in (0, 1):
            back_copy(g, direction, 0).start()

    def pass_back(g, h):
        for direction in (0, 1):
            count = counts(g)[direction]
            if h < count - 1:
                buffers = (ring_up, ring_down)[direction]
                back_copy(g, direction, h).wait_recv()
                dest = z + (count - 1 - h) if direction == 0 else z - (count - 1 - h)
                buffers[g, h] = (buffers[g, h].astype(F32) + dense[g, block(dest)].astype(F32)).astype(BF16)
                back_copy(g, direction, h + 1).start()

    def row_copy(g, k, source):
        piece = rows.at[source, g]
        return remote(piece, piece, row_sems.at[0, g, k - 1], row_sems.at[1, g, k - 1], peer(k))

    def settle(g):
        n_up, n_down = counts(g)
        back_copy(g, 0, n_up - 1).wait_recv()
        back_copy(g, 1, n_down - 1).wait_recv()
        whole = dense[g, block(z)].astype(F32) + ring_up[g, n_up - 1].astype(F32) + ring_down[g, n_down - 1].astype(F32)
        rows[y, g] = whole.astype(BF16).reshape(256, HEAD)
        for k in ORDER:
            row_copy(g, k, y).start()

    def sum_copy(g, direction, n):
        buffers, firsts, target = ((sum_up, first_up, up), (sum_down, first_down, down))[direction]
        src = firsts.at[g] if n == 0 else buffers.at[g, n - 1]
        return remote(src, buffers.at[g, n], sum_sems.at[0, g, direction, n], sum_sems.at[1, g, direction, n], target)

    def weigh(g):
        for k in ORDER:
            row_copy(g, k, from_y(k)).wait_recv()
        row_grad = jnp.concatenate([rows[s, g] for s in range(NY)], axis=0)

        def partial_of(dest):
            return jnp.dot(normed[wrap(dest, NZ)], row_grad, preferred_element_type=F32)

        n_up, n_down = counts(g)
        for direction in (g % 2, 1 - g % 2):
            if direction == 0:
                first_up[g] = partial_of(z + n_up).astype(BF16)
            else:
                first_down[g] = partial_of(z - n_down).astype(BF16)
            sum_copy(g, direction, 0).start()
        for offset in (3, -3, 2, -2, 1, -1, 0):
            if offset not in (n_up, -n_down):
                parts[g, wrap(z + offset, NZ)] = partial_of(z + offset)

    def pass_sum(g, n):
        for direction in (g % 2, 1 - g % 2):
            count = counts(g)[direction]
            if n < count - 1:
                buffers = (sum_up, sum_down)[direction]
                sum_copy(g, direction, n).wait_recv()
                dest = z + (count - 1 - n) if direction == 0 else z - (count - 1 - n)
                buffers[g, n] = (buffers[g, n].astype(F32) + parts[g, wrap(dest, NZ)]).astype(BF16)
                sum_copy(g, direction, n + 1).start()

    def weights_out(g):
        n_up, n_down = counts(g)
        sum_copy(g, 0, n_up - 1).wait_recv()
        sum_copy(g, 1, n_down - 1).wait_recv()
        whole = parts[g, z] + sum_up[g, n_up - 1].astype(F32) + sum_down[g, n_down - 1].astype(F32)
        done_weights[g] = whole
        weight_out(g).start()

    def weight_out(g):
        ref = (vw_hbm, kw_hbm)[g // 2]
        return pltpu.make_async_copy(done_weights.at[g], ref.at[:, pl.ds(HEAD * (g % 2), HEAD)], out_sems.at[4 + g])

    def arrive(k):
        store_copy(k, from_y(k), (z, y, m)).wait_recv()
        pieces[k].step(0)

    def send_queries():
        for h in range(2):
            for k in ORDER:
                for i in range(2):
                    qo_copy(h, i, k, y).start()

    def weights_here():
        for k in range(1, NM):
            gain_copy(k, wrap(m - k, NM), m).wait_recv()
        home[1].wait()
        home[2].wait()

    def finish_piece(k):
        pieces[k].step(4)
        encode(k)
        launch(k, 0)
        launch(k, 1)

    go = functools.partial
    plan = [(4.3, go(arrive, 1)), (4.5, go(arrive, 3)), (6.3, go(arrive, 2)), (6.4, send_queries), (7.0, weights_here), (17.2, turn)]
    for k, steps in ((0, (3.7, 4.4, 6.8, 8.2)), (1, (8.0, 8.7, 11.0, 12.5)), (3, (8.6, 9.3, 11.7, 13.3)), (2, (10.5, 11.2, 13.5, 15.0))):
        for number in range(3):
            plan.append((steps[number], go(pieces[k].step, number + 1)))
        plan.append((steps[3], go(finish_piece, k)))
        for h in range(4):
            due = steps[3] + 2.0 + 3.4 * (h + 1)
            plan.append((due, go(advance, k, 0, h)))
            plan.append((due + 2.0, go(advance, k, 1, h)))

    def scalars_here():
        for k in ORDER:
            tab_copy(k, from_y(k)).wait_recv()
        to_scalars = pltpu.make_async_copy(table, table_s, local.at[7])
        to_scalars.start()
        for copy in home[5:]:
            copy.wait()
        to_scalars.wait()

    def queries_here(h):
        for i in range(2):
            for k in ORDER:
                qo_copy(h, i, k, from_y(k)).wait_recv()

    def send_stats():
        for k in ORDER:
            stat_copy(k, y).start()

    def stats_here():
        for k in ORDER:
            stat_copy(k, from_y(k)).wait_recv()

    def send_moments():
        for k in ORDER:
            moment_copy(k, y).start()

    def moments_here():
        for k in ORDER:
            moment_copy(k, from_y(k)).wait_recv()

    def turned_here():
        for k in ORDER:
            turn_copy(k, from_y(k)).wait_recv()

    due = 15.0 + 2.0 + 3.4 * 4 + 0.1
    plan += [(due, scalars_here), (due, go(queries_here, 0)), (due, go(queries_here, 1))]
    plan += [(due, go(score, h, k)) for h in range(2) for k in range(NY)] + [(due, send_stats)]
    steps = [action for _, action in sorted(plan, key=lambda entry: entry[0])]
    steps += [stats_here] + [go(attend, 0, k) for k in range(NY)] + [go(add_up, 0)]
    steps += [go(attend, 1, k) for k in range(NY)] + [send_moments, go(add_up, 1), go(send_parts, 0, 0), go(send_parts, 1, 0)]
    steps += [turned_here, go(second_moves.step, 0), go(pass_back, 0, 0), go(pass_back, 1, 0), moments_here]
    for h in range(2):
        steps += [go(grads_of, h, k) for k in range(NY)] + [go(add_up, 2 + h)]
    steps += [go(send_parts, 0, 1), go(pass_back, 0, 1), go(pass_back, 1, 1)]
    steps += [go(pass_back, 2, 0), go(pass_back, 3, 0), go(pass_back, 0, 2), go(pass_back, 1, 2), go(second_moves.step, 1), go(second_moves.step, 2)]
    steps += [go(pass_back, 2, 1), go(pass_back, 3, 1), go(settle, 0), go(settle, 1), go(second_moves.step, 3)]
    steps += [go(pass_back, 2, 2), go(pass_back, 3, 2), go(second_moves.step, 4), go(settle, 2), go(weigh, 0), go(settle, 3)]
    steps += [go(weigh, 1), go(pass_sum, 0, 0), go(outputs, 0, 0), go(outputs, 1, 0), go(pass_sum, 1, 0)]
    steps += [go(weigh, 2), go(pass_sum, 0, 1), go(pass_sum, 1, 1), go(weigh, 3), go(send_parts, 1, 1), go(pass_sum, 0, 2), go(pass_sum, 1, 2)]
    steps += [go(pass_sum, 2, 0), go(pass_sum, 3, 0), go(weights_out, 0), go(weights_out, 1), go(pass_sum, 2, 1), go(pass_sum, 3, 1)]
    steps += [go(outputs, 0, 1), go(pass_sum, 2, 2), go(pass_sum, 3, 2), go(weights_out, 2), go(weights_out, 3), go(outputs, 1, 1)]
    for action in steps:
        action()

    for moves in pieces + [second_moves]:
        moves.finish()
    for h in range(2):
        for i in range(2):
            part_out(h, i).wait()
    for g in range(4):
        weight_out(g).wait()
    for k in ORDER:
        store_copy(k, y, peer(k)).wait_send()
        tab_copy(k, y).wait_send()
        turn_copy(k, y).wait_send()
        stat_copy(k, y).wait_send()
        moment_copy(k, y).wait_send()
        for h in range(2):
            for i in range(2):
                qo_copy(h, i, k, y).wait_send()
                part_copy(h, i, k).wait_send()
        for g in range(4):
            row_copy(g, k, y).wait_send()
    for k in range(1, NM):
        gain_copy(k, m, wrap(m + k, NM)).wait_send()
    for direction in (0, 1):
        for g in range(4):
            for n in range(counts(g)[direction]):
                ring_sent(g, 0, direction, n).wait_send()
                ring_sent(g, 1, direction, n).wait_send()
                back_copy(g, direction, n).wait_send()
                sum_copy(g, direction, n).wait_send()


def hand_over(*refs):
    for source, target in zip(refs[:4], refs[4:]):
        target[...] = source[...]


def dma(*shape):
    return pltpu.SemaphoreType.DMA(shape)


def shards(queries, out_grad, owner, store_row, store, norm_gain, w_key, w_value):
    in_vmem, anywhere = (pl.BlockSpec(memory_space=space) for space in (VMEM, pl.ANY))
    tile = (TOK, HEAD)
    results = pl.pallas_call(
        kernel,
        out_shape=(
            jax.ShapeDtypeStruct((512, 256), BF16),
            jax.ShapeDtypeStruct((512, 256), BF16),
            jax.ShapeDtypeStruct((128, 256), F32),
            jax.ShapeDtypeStruct((128, 256), F32),
        ),
        in_specs=[anywhere, anywhere, anywhere, anywhere, anywhere, in_vmem, anywhere, anywhere],
        out_specs=(anywhere,) * 4,
        scratch_shapes=[
            SMEM((2, 8), I32),
            SMEM((2, 8), I32),
            VMEM((2, 2, 512, HEAD), BF16),
            VMEM((4, 128, HEAD), F32),
            VMEM((NM, 8, TOK, 512), BF16),
            VMEM((NM, 8, TOK, 512), BF16),
            VMEM((NM, 16, 512), BF16),
            VMEM((4096, 256), BF16),
            VMEM((4096, 256), BF16),
            VMEM((NY, 8, 128), I32),
            SMEM((NY, 8, 128), I32),
            VMEM((2, NY, 2, 512, HEAD), BF16),
            VMEM((NY, 128, 256), BF16),
            VMEM((NM, 128, 1024), BF16),
            VMEM((2, 64) + tile, BF16),
            VMEM((2, 64) + tile, BF16),
            VMEM((2, NY, 4, 128, 128), F32),
            VMEM((2, NY, 4, 128, 128), F32),
            VMEM((NY, 2, NY, 8, 128), F32),
            VMEM((NY, 2, NY, 8, 128), F32),
            VMEM((2, 2, 512, HEAD), F32),
            VMEM((2, 2, 3, 512, HEAD), BF16),
            VMEM((2, 2, 3, 512, HEAD), BF16),
        ]
        + [VMEM((NY, REFS + 1) + tile, F32)] * 4
        + [
            VMEM((4, 64) + tile, BF16),
            VMEM((4, 4, 8) + tile, BF16),
            VMEM((4, 4, 8) + tile, BF16),
            VMEM((NY, 4, 256, HEAD), BF16),
            VMEM((4, NZ, 128, HEAD), F32),
            VMEM((4, 128, HEAD), BF16),
            VMEM((4, 128, HEAD), BF16),
            VMEM((4, 4, 128, HEAD), BF16),
            VMEM((4, 4, 128, HEAD), BF16),
            dma(11), dma(8), dma(2, 3), dma(2, 7), dma(2, 3), dma(2, 2, 2, 3), dma(4, 11), dma(4, 11), dma(2, 3), dma(1, 11), dma(1, 11),
            dma(2, 8, 2, 4), dma(2, 3), dma(2, 3), dma(2, 4, 2, 4), dma(2, 2, 2, 3), dma(2, 4, 3), dma(2, 4, 2, 4),
        ],
        compiler_params=pltpu.CompilerParams(
            collective_id=0, has_side_effects=True, vmem_limit_bytes=60 * 1024 * 1024
        ),
        name="spans",
    )(owner.T, store_row.T, queries, out_grad, store, norm_gain, w_key, w_value)
    return pl.pallas_call(
        hand_over,
        out_shape=tuple(jax.ShapeDtypeStruct(each.shape, each.dtype) for each in results),
        in_specs=[in_vmem] * 4,
        out_specs=(in_vmem,) * 4,
        name="hand_over",
    )(*results)


def solution(mesh):
    in_specs = (
        P("dp", "mp"),
        P("dp", "mp"),
        P("dp", None),
        P("dp", None),
        P("dp", None, "mp"),
        P("mp"),
        P(None, "mp"),
        P(None, "mp"),
    )
    out_specs = (P("dp", "mp"), P("dp", "mp"), P("dp", "mp"), P("dp", "mp"))
    return jax.shard_map(shards, mesh=mesh, in_specs=in_specs, out_specs=out_specs, check_vma=False)
```
